32 devices in a mesh: groups: 2 (over x), dp: 16 (over z, y, core).
Axes of the slice: x: 2, y: 2, z: 4, core: 2. Of those that a mesh axis runs over, the one named last changes fastest.
Arguments:
- tokens: bfloat16 [4096, 8192], P(('groups', 'dp')), parts along dimension 0, may hold values from -6 to 6
- out_grad: bfloat16 [4096, 512], P(('groups', 'dp')), parts along dimension 0, may hold values from -6 to 6
- base_weight: bfloat16 [8192, 512], P('dp'), may hold values from -0.0625 to 0.0625
- adapter_down: bfloat16 [16, 64, 8192], P(None, None, 'dp'), may hold values from -0.0625 to 0.0625
- adapter_up: bfloat16 [16, 32768], P(None, 'dp'), may hold values from -0.75 to 0.75
- rank_tiles: int32 [16], replicated, may hold values from 1 to 4, as said below
- tile_adapter: int32 [32, 1], P('groups'), parts along dimension 0, may hold values from 0 to 15
Outputs:
- result: bfloat16 [4096, 512], P(('groups', 'dp')), parts along dimension 0
- grad_in: bfloat16 [4096, 8192], P(('groups', 'dp')), parts along dimension 0
- down_grad: bfloat16 [32, 64, 8192], P('groups', None, 'dp'), parts along dimension 0
- up_grad: bfloat16 [32, 32768], P('groups', 'dp'), parts along dimension 0
The draws below stay inside these ranges and needn't reach their ends.
There are 2 independent parts, one for each index of `groups`. The reference program is written for one: setup_inputs(seed, part) draws one part's arguments, and reference() takes and returns one part's arrays. A program takes and returns all parts, laid end to end along the dimension named above; an argument that names none is the same for every part. Nothing has to cross between parts.
Inputs may be any that keep to these rules, and one draw needn't show every extreme that they name: `rank_tiles`: ranks of 1 and of 4 tiles occur in every draw. `tile_adapter`: every adapter is used by at least one tile.
All inputs are finite; a program needn't handle non-finite values.
Results may differ from the reference program's by a relative error of at most 0.005.
Values may be sent and summed in bfloat16 or wider, within the bound.
No kernel may reach another device: no remote copies, remote signals or barrier semaphores. Data moves between devices by JAX's collectives and lax.ppermute only.
A program may use at most 64 MiB of HBM per device.

```python
import jax
import jax.numpy as jnp
from jax import lax

D = 8192
DOUT = 512
RANK_TILE = 16
RMAX = 64
TILE = 128
TOKENS = 2048
TILES_ALL = 16
ADAPTERS = 16


def draw_rank_tiles(key, part):
    key = jax.random.fold_in(key, 7)
    first_key, second_key, third_key = jax.random.split(key, 3)
    values = jax.random.randint(first_key, (ADAPTERS,), 1, 5)
    high_spot = jax.random.randint(second_key, (), 0, ADAPTERS)
    low_spot = (high_spot + 1 + jax.random.randint(third_key, (), 0, ADAPTERS - 1)) % ADAPTERS
    values = values.at[high_spot].set(4)
    values = values.at[low_spot].set(1)
    return values.astype(jnp.int32)


def block_scale(rng, dims, cuts, smallest, largest):
    gain = 1.0
    for position, shards_of in cuts:
        draws = jax.random.uniform(jax.random.fold_in(jax.random.fold_in(rng, 6), position), (shards_of,), jnp.float32, smallest / len(cuts), largest / len(cuts))
        gain = gain * jnp.repeat(jnp.exp(draws), dims[position] // shards_of).reshape((-1,) + (1,) * (len(dims) - 1 - position))
    return gain


def different_ones(own_key, rows, count, top, lift):
    order = jax.random.permutation(jax.random.fold_in(own_key, 1), count)
    favour = order
    for power in range(3):
        favour = favour * favour // count
    favour = favour * lift // count
    tickets = jax.random.randint(jax.random.fold_in(own_key, 2), (rows, count), 0, 4096) + favour
    holders = jax.random.permutation(jax.random.fold_in(own_key, 3), rows)[jnp.arange(count) % rows]
    tickets = jnp.where(jnp.arange(rows)[:, None] == holders[None, :], 1 << 14, tickets)
    score = tickets * count + jnp.arange(count)
    return lax.top_k(score.astype(jnp.int32), top)[1].astype(jnp.int32)


def gaussian(own_key, extent, deviation, reach, shards=(), kind=jnp.bfloat16):
    entries = deviation * jax.random.normal(own_key, extent, jnp.float32)
    if shards:
        entries = entries * block_scale(own_key, extent, shards, -0.22, 0.18)
    return jnp.clip(entries, -reach, reach).astype(kind)


def setup_inputs(seed: int = 0, part: int = 0) -> dict:
    key_list = jax.random.split(jax.random.key(seed), 8)
    part_splits = jax.random.split(jax.random.fold_in(key_list[7], part), 8)
    return {
        "tokens": gaussian(part_splits[0], (TOKENS, D), 1.0, 6.0, ((0, 16),)),
        "out_grad": gaussian(part_splits[1], (TOKENS, DOUT), 1.0, 6.0, ((0, 16),)),
        "base_weight": gaussian(key_list[2], (D, DOUT), D ** -0.5, 0.0625, ((0, 16),)),
        "adapter_down": gaussian(key_list[3], (ADAPTERS, RMAX, D), D ** -0.5, 0.0625, ((2, 16),)),
        "adapter_up": gaussian(key_list[4], (ADAPTERS, DOUT * RMAX), RMAX ** -0.5, 0.75, ((1, 16),)),
        "rank_tiles": draw_rank_tiles(jax.random.fold_in(key_list[7], 71), part),
        "tile_adapter": different_ones(part_splits[6], TILES_ALL, ADAPTERS, 1, 1024),
    }


def reference(tokens, out_grad, base_weight, adapter_down, adapter_up, rank_tiles, tile_adapter):
    tile_ids = tile_adapter[:, 0].astype(jnp.int32)
    token_blocks = tokens.reshape(TILES_ALL, TILE, D)
    grad_blocks = out_grad.reshape(TILES_ALL, TILE, DOUT)
    columns = jnp.arange(RMAX, dtype=jnp.int32)

    def one_tile(carried, element):
        down_sum, up_sum = carried
        token_tile, grad_tile, adapter = element
        down_rows = adapter_down[adapter]
        up_matrix = adapter_up[adapter].reshape(DOUT, RMAX)
        tile_count = rank_tiles[adapter]
        factor = (columns < tile_count * RANK_TILE).astype(jnp.float32) * (2.0 / tile_count.astype(jnp.float32))
        lowrank = jnp.dot(token_tile, down_rows.T, preferred_element_type=jnp.float32)
        hidden = (lowrank * factor[None, :]).astype(jnp.bfloat16)
        output = jnp.dot(token_tile, base_weight, preferred_element_type=jnp.float32)
        output = (output + jnp.dot(hidden, up_matrix.T, preferred_element_type=jnp.float32)).astype(jnp.bfloat16)
        backward = jnp.dot(grad_tile, up_matrix, preferred_element_type=jnp.float32)
        backward = (backward * factor[None, :]).astype(jnp.bfloat16)
        input_low = jnp.dot(backward, down_rows, preferred_element_type=jnp.float32).astype(jnp.bfloat16)
        input_low = lax.optimization_barrier(input_low)
        grad_input = jnp.dot(grad_tile, base_weight.T, preferred_element_type=jnp.float32)
        grad_input = (grad_input + input_low.astype(jnp.float32)).astype(jnp.bfloat16)
        down_sum = down_sum.at[adapter].add(jnp.dot(backward.T, token_tile, preferred_element_type=jnp.float32))
        up_term = jnp.dot(grad_tile.T, hidden, preferred_element_type=jnp.float32).reshape(DOUT * RMAX)
        up_sum = up_sum.at[adapter].add(up_term)
        return (down_sum, up_sum), (output, grad_input)

    initial = (jnp.zeros((ADAPTERS, RMAX, D), jnp.float32), jnp.zeros((ADAPTERS, DOUT * RMAX), jnp.float32))
    (down_sum, up_sum), (outputs, grad_inputs) = lax.scan(one_tile, initial, (token_blocks, grad_blocks, tile_ids))
    return (outputs.reshape(TOKENS, DOUT), grad_inputs.reshape(TOKENS, D),
            down_sum.astype(jnp.bfloat16), up_sum.astype(jnp.bfloat16))
```

```python
import jax
import jax.numpy as jnp
from jax import lax
from jax.sharding import PartitionSpec as P

RANK_TILE = 16


def body(tokens, out_grad, base_weight, adapter_down, adapter_up, rank_tiles, tile_adapter):
    rows, model_width = tokens.shape
    out_width = out_grad.shape[1]
    adapters, rank_width, slice_width = adapter_down.shape
    all_ids = tile_adapter[:, 0]
    tiles = all_ids.shape[0]
    position = lax.axis_index("dp")
    holder = jnp.argsort(all_ids)
    my_tiles = rank_tiles[all_ids[position]]
    columns = jnp.arange(rank_width, dtype=jnp.int32)
    factor = jnp.where(columns < my_tiles * RANK_TILE, 2.0 / my_tiles.astype(jnp.float32), 0.0)

    weight = lax.all_gather(base_weight, "dp", axis=0, tiled=True)
    up_mine = lax.all_to_all(adapter_up[all_ids], "dp", split_axis=0, concat_axis=0, tiled=True)
    up_mine = up_mine.reshape(out_width, rank_width)
    down_mine = lax.all_to_all(adapter_down[all_ids], "dp", split_axis=0, concat_axis=0, tiled=True)

    backward = jnp.dot(out_grad, up_mine, preferred_element_type=jnp.float32)
    backward = (backward * factor[None, :]).astype(jnp.bfloat16)
    token_cols = tokens.reshape(rows, tiles, slice_width)
    down_term = jnp.einsum("sr,std->trd", backward, token_cols, preferred_element_type=jnp.float32)
    down_back = lax.all_to_all(
        down_term.astype(jnp.bfloat16), "dp", split_axis=0, concat_axis=0, tiled=True
    )
    down_grad = down_back[holder]

    lowrank = jnp.einsum("std,trd->sr", token_cols, down_mine, preferred_element_type=jnp.float32)
    hidden = (lowrank * factor[None, :]).astype(jnp.bfloat16)
    up_term = jnp.dot(out_grad.T, hidden, preferred_element_type=jnp.float32).astype(jnp.bfloat16)
    up_back = lax.all_to_all(
        up_term.reshape(tiles, -1), "dp", split_axis=0, concat_axis=0, tiled=True
    )
    up_grad = up_back[holder]
    out_low = jnp.dot(hidden, up_mine.T, preferred_element_type=jnp.float32)
    in_low = jnp.einsum("sr,trd->std", backward, down_mine, preferred_element_type=jnp.float32)
    in_low = in_low.astype(jnp.bfloat16).reshape(rows, model_width)

    forward = jnp.dot(tokens, weight, preferred_element_type=jnp.float32)
    grad_cols = jnp.dot(out_grad, weight.T, preferred_element_type=jnp.float32)
    result = (forward + out_low).astype(jnp.bfloat16)
    grad_in = (grad_cols + in_low.astype(jnp.float32)).astype(jnp.bfloat16)
    return result, grad_in, down_grad, up_grad


def solution(mesh):
    return jax.shard_map(
        body,
        mesh=mesh,
        in_specs=(
            P(("groups", "dp"), None),
            P(("groups", "dp"), None),
            P("dp", None),
            P(None, None, "dp"),
            P(None, "dp"),
            P(),
            P("groups", None),
        ),
        out_specs=(
            P(("groups", "dp"), None),
            P(("groups", "dp"), None),
            P("groups", None, "dp"),
            P("groups", "dp"),
        ),
        check_vma=False,
    )
```

```python
import functools

import jax
import jax.numpy as jnp
from jax import lax
from jax.experimental import pallas as pl
from jax.experimental.pallas import tpu as pltpu
from jax.sharding import PartitionSpec as P

RANK_TILE = 16
AXES = ("groups", "dp")
F32 = jnp.float32
BF16 = jnp.bfloat16
VMEM = pl.BlockSpec(memory_space=pltpu.VMEM)
SMEM = pl.BlockSpec(memory_space=pltpu.SMEM)


def dot(a, b, ca, cb):
    return lax.dot_general(a, b, (((ca,), (cb,)), ((), ())), preferred_element_type=F32)


def call(kernel, outs, scalars, arrays, flops=0):
    size = sum(x.size * x.dtype.itemsize for x in arrays)
    size += sum(x.size * x.dtype.itemsize for x in outs)
    return pl.pallas_call(
        kernel,
        out_shape=outs,
        in_specs=[SMEM] * len(scalars) + [VMEM] * len(arrays),
        out_specs=[VMEM] * len(outs),
        compiler_params=pltpu.CompilerParams(vmem_limit_bytes=40 * 1024 * 1024),
        cost_estimate=pl.CostEstimate(flops=flops, bytes_accessed=size, transcendentals=0),
    )(*scalars, *arrays)


def shape(dims, dtype=BF16):
    return jax.ShapeDtypeStruct(dims, dtype)


def iota(dims, axis):
    return lax.broadcasted_iota(jnp.int32, dims, axis)


def factor_of(ids, ranks, tile, width):
    count = ranks[ids[tile]]
    scale = 2.0 / jnp.full((1, width), count, jnp.int32).astype(F32)
    return jnp.where(iota((1, width), 1) < count * RANK_TILE, scale, 0.0)


def pack_kernel(chips, meta, ids, down, up_own, up_other, *blocks):
    adapters, rank, width = down.shape
    k, c = meta[0], meta[1]
    rows = chips * 16
    q = iota((rows, adapters), 0)
    chosen = jnp.zeros((rows, adapters), jnp.int32)
    for j in range(chips):
        for slot in range(2):
            adapter = ids[2 * jnp.bitwise_xor(k, j) + jnp.bitwise_xor(c, slot)]
            blocks[j][rank * slot : rank * (slot + 1), :] = down[adapter]
            chosen = jnp.where(q // 8 == 2 * j + slot, adapter, chosen)
    match = chosen == iota((rows, adapters), 1)
    packed = jnp.zeros((rows, width), F32)
    for side, up in enumerate((up_own, up_other)):
        for r in range(4):
            pick = (match & (q % 8 == 4 * side + r)).astype(F32).astype(BF16)
            packed = packed + dot(pick, up[:, width * r : width * (r + 1)], 1, 0)
    packed = packed.astype(BF16)
    for j in range(chips):
        blocks[j][2 * rank : 2 * rank + 16, :] = packed[16 * j : 16 * (j + 1), :]


def rank_kernel(chips, meta, ids, ranks, tok_own, tok_sib, og_own, og_sib, *refs):
    blocks, outs = refs[:chips], refs[chips:]
    grads, (low_own, low_sib, back_own, back_sib, up_out) = outs[:chips], outs[chips:]
    width = blocks[0].shape[1]
    out_width = og_own.shape[1]
    rank = back_own.shape[1]
    k, c = meta[0], meta[1]
    heads = out_width // (2 * chips)
    per_row = width // rank
    packed = jnp.concatenate([b[2 * rank : 2 * rank + 16, :] for b in blocks], axis=0)
    q = iota((out_width, chips * 16), 1)
    o = iota((out_width, chips * 16), 0)
    device = 2 * jnp.bitwise_xor(k, q // 16) + jnp.bitwise_xor(c, (q // 4) % 2)
    place = o // per_row == device * (heads // per_row) + q % 4
    lane_ok = iota((out_width, width), 1) // rank == iota((out_width, width), 0) % per_row
    fold = (iota((width, rank), 0) % rank == iota((width, rank), 1)).astype(F32).astype(BF16)
    for slot, (tok, og, low, back) in enumerate(
        ((tok_own, og_own, low_own, back_own), (tok_sib, og_sib, low_sib, back_sib))
    ):
        pick = (place & ((q // 8) % 2 == slot)).astype(F32).astype(BF16)
        spread = jnp.where(lane_ok, dot(pick, packed, 1, 0), 0.0).astype(BF16)
        up = dot(spread, fold, 1, 0).astype(BF16)
        if slot == 0:
            up_out[...] = up
        factor = factor_of(ids, ranks, 2 * k + jnp.bitwise_xor(c, slot), rank)
        backward = (dot(og[...], up, 1, 0) * factor).astype(BF16)
        back[...] = backward
        turned = backward.T
        total = jnp.zeros((tok.shape[0], rank), F32)
        for j in range(chips):
            start = pl.multiple_of((2 * jnp.bitwise_xor(k, j) + c) * width, width)
            part = tok[:, pl.ds(start, width)]
            grads[j][rank * slot : rank * (slot + 1), :] = dot(turned, part, 1, 0).astype(BF16)
            total = total + dot(part, blocks[j][rank * slot : rank * (slot + 1), :], 1, 1)
        low[...] = total


def hidden_kernel(meta, ids, ranks, low_mine, low_other, og, up, up_term, out_low):
    rank = up.shape[1]
    out_width = og.shape[1]
    factor = factor_of(ids, ranks, 2 * meta[0] + meta[1], rank)
    hidden = ((low_mine[...] + low_other[...]) * factor).astype(BF16)
    out_low[...] = dot(hidden, up[...], 1, 1)
    term = dot(og[...], hidden, 0, 0).astype(BF16)
    half = out_width // 2
    total = jnp.zeros((half, 2 * rank), F32)
    for odd in range(2):
        pick = (iota((half, out_width), 1) == 2 * iota((half, out_width), 0) + odd)
        move = (iota((rank, 2 * rank), 1) == iota((rank, 2 * rank), 0) + odd * rank)
        rows = dot(pick.astype(F32).astype(BF16), term, 1, 0).astype(BF16)
        total = total + dot(rows, move.astype(F32).astype(BF16), 1, 0)
    up_term[...] = total.astype(BF16).reshape(up_term.shape)


def base_kernel(chips, plan, meta, tok_own, tok_sib, og_own, og_sib, back_own, back_sib, *refs):
    blocks = refs[:chips]
    pieces = refs[chips : len(refs) - 4]
    for_own, for_sib, grad_own, grad_sib = refs[len(refs) - 4 :]
    width = blocks[0].shape[1]
    rank = back_own.shape[1]
    rows = tok_own.shape[0]
    k, c, g = meta[0], meta[1], meta[2]
    og = jnp.concatenate([og_own[...], og_sib[...]], axis=0)
    total = jnp.zeros((2 * rows, og.shape[1]), F32)
    for piece, (j, count, side, whole) in zip(pieces, plan):
        chip = jnp.bitwise_xor(k, j)
        shift = 0 if side is None else jnp.bitwise_xor(g, side) * count
        if whole:
            weight = piece[pl.ds(pl.multiple_of(chip * count, count), count), :]
        else:
            weight = piece[...]
        start = pl.multiple_of((2 * chip + c) * width + shift, 128)
        tok = jnp.concatenate(
            [tok_own[:, pl.ds(start, count)], tok_sib[:, pl.ds(start, count)]], axis=0
        )
        total = total + dot(tok, weight, 1, 0)
        grad = dot(og, weight, 1, 1)
        inner = pl.ds(pl.multiple_of(shift, 128), count)
        low_own = dot(back_own[...], blocks[j][0:rank, inner], 1, 0).astype(BF16)
        low_sib = dot(back_sib[...], blocks[j][rank : 2 * rank, inner], 1, 0).astype(BF16)
        to = pl.ds(pl.multiple_of(chip * width + shift, 128), count)
        grad_own[:, to] = (grad[:rows] + low_own.astype(F32)).astype(BF16)
        grad_sib[:, to] = (grad[rows:] + low_sib.astype(F32)).astype(BF16)
    for_own[...] = total[:rows]
    for_sib[...] = total[rows:]


def join_kernel(chips, meta, mine, other, out_low, grad_mine, grad_other, result, grad_in):
    c = meta[1]
    result[...] = (mine[...] + other[...] + out_low[...]).astype(BF16)
    width = grad_mine.shape[1] // chips
    for chip in range(chips):
        cols = slice(width * chip, width * (chip + 1))
        own = pl.multiple_of((2 * chip + c) * width, width)
        sib = pl.multiple_of((2 * chip + 1 - c) * width, width)
        grad_in[:, pl.ds(own, width)] = grad_mine[:, cols]
        grad_in[:, pl.ds(sib, width)] = grad_other[:, cols]


def down_kernel(chips, meta, ids, *refs):
    out = refs[-1]
    rank = out.shape[1]
    k, c = meta[0], meta[1]
    for j in range(chips):
        for slot in range(2):
            adapter = ids[2 * jnp.bitwise_xor(k, j) + jnp.bitwise_xor(c, slot)]
            out[adapter] = refs[j][rank * slot : rank * (slot + 1), :]


def up_kernel(ids, back, out):
    tiles, rows, lanes = back.shape
    flat = back[...].reshape(tiles * rows, lanes)
    q = iota((out.shape[0], tiles * rows), 1)
    chosen = jnp.zeros(q.shape, jnp.int32)
    for tile in range(tiles):
        chosen = jnp.where(q // rows == tile, ids[tile], chosen)
    match = chosen == iota(q.shape, 0)
    for row in range(rows):
        pick = (match & (q % rows == row)).astype(F32).astype(BF16)
        out[:, lanes * row : lanes * (row + 1)] = dot(pick, flat, 1, 0).astype(BF16)


def pairs(groups, size, to):
    out = []
    for g in range(groups):
        for d in range(size):
            target = to(g, d)
            if target is not None:
                out.append((g * size + d, target[0] * size + target[1]))
    return out


def gather_weight(weight, groups, size, send):
    chips = size // 2
    rows = weight.shape[0]
    if groups != 2 or chips != 8:
        lists = [[2 * chip + core for chip in range(chips)] for core in range(2)]
        full = lax.all_gather(weight, "dp", axis=0, tiled=True, axis_index_groups=lists)
        return [(full, (j, rows, None, True)) for j in range(chips)]
    half = rows // 2
    place = lax.axis_index("dp")
    z = place // 4
    middle = (z == 1) | (z == 2)
    mine = lax.dynamic_slice_in_dim(weight, lax.axis_index("groups") * half, half)
    swap_x = lambda g, d: (1 - g, d)
    swap_y = lambda g, d: (g, d ^ 2)
    swap_near = lambda g, d: (g, d ^ 4)
    swap_mid = lambda g, d: (g, d ^ 12) if d // 4 in (1, 2) else None
    outward = lambda g, d: (g, d ^ 4) if d // 4 in (1, 2) else None
    near = send(mine, swap_near)
    cross = send(mine, swap_mid)
    own_y = send(weight, swap_y)
    cross_near = send(near, swap_mid)
    edge = send(cross, outward)
    edge_near = send(cross_near, outward)
    by_slot = (
        (2, near),
        (4, jnp.where(middle, cross_near, edge)),
        (6, jnp.where(middle, cross, edge_near)),
    )
    pieces = [(weight, (0, rows, None, False)), (own_y, (1, rows, None, False))]
    for j, held in by_slot:
        over_y = send(held, swap_y)
        pieces.append((held, (j, half, 0, False)))
        pieces.append((send(held, swap_x), (j, half, 1, False)))
        pieces.append((over_y, (j + 1, half, 0, False)))
        pieces.append((send(over_y, swap_x), (j + 1, half, 1, False)))
    return pieces


def body(groups, size, tokens, out_grad, base_weight, adapter_down, adapter_up, rank_tiles, tile_adapter):
    chips = size // 2
    rows, model_width = tokens.shape
    out_width = out_grad.shape[1]
    adapters, rank, width = adapter_down.shape
    ids = tile_adapter[:, 0]
    place = lax.axis_index("dp")
    meta = jnp.stack([place // 2, place % 2, lax.axis_index("groups")]).astype(jnp.int32)

    def send(x, to):
        return lax.ppermute(x, AXES, pairs(groups, size, to))

    def sibling(x):
        return send(x, lambda g, d: (g, d ^ 1))

    def exchange(blocks):
        moved = [blocks[0]] + [None] * (chips - 1)
        for j in reversed(range(1, chips)):
            moved[j] = send(blocks[j], lambda g, d: (g, d ^ (2 * j)))
        return moved

    up_sib = sibling(adapter_up)
    tok_sib = sibling(tokens)
    og_sib = sibling(out_grad)
    block = shape((2 * rank + 16, width))
    packed = call(
        functools.partial(pack_kernel, chips),
        [block] * chips,
        (meta, ids),
        (adapter_down, adapter_up, up_sib),
    )
    blocks = exchange(packed)
    pieces = gather_weight(base_weight, groups, size, send)

    *grads, low_own, low_sib, back_own, back_sib, up_mine = call(
        functools.partial(rank_kernel, chips),
        [shape((2 * rank, width))] * chips
        + [shape((rows, rank), F32)] * 2
        + [shape((rows, rank))] * 2
        + [shape((out_width, rank))],
        (meta, ids, rank_tiles),
        (tokens, tok_sib, out_grad, og_sib, *blocks),
        flops=4 * rows * model_width * rank,
    )
    grads_back = exchange(grads)
    low_other = sibling(low_sib)
    up_rows = adapter_up.shape[1] // (2 * rank)
    up_term, out_low = call(
        hidden_kernel,
        [shape((size, up_rows, 2 * rank)), shape((rows, out_width), F32)],
        (meta, ids, rank_tiles),
        (low_own, low_other, out_grad, up_mine),
        flops=4 * rows * out_width * rank,
    )
    up_back = lax.all_to_all(up_term, "dp", split_axis=0, concat_axis=0, tiled=True)
    (up_grad,) = call(up_kernel, [shape(adapter_up.shape)], (ids,), (up_back,))

    for_own, for_sib, grad_own, grad_sib = call(
        functools.partial(base_kernel, chips, [p[1] for p in pieces]),
        [shape((rows, out_width), F32)] * 2 + [shape((rows, model_width // 2))] * 2,
        (meta,),
        (tokens, tok_sib, out_grad, og_sib, back_own, back_sib, *blocks, *[p[0] for p in pieces]),
        flops=4 * rows * model_width * out_width,
    )
    for_other, grad_other = sibling(for_sib), sibling(grad_sib)
    result, grad_in = call(
        functools.partial(join_kernel, chips),
        [shape((rows, out_width)), shape((rows, model_width))],
        (meta,),
        (for_own, for_other, out_low, grad_own, grad_other),
    )
    (down_grad,) = call(
        functools.partial(down_kernel, chips),
        [shape(adapter_down.shape)],
        (meta, ids),
        tuple(grads_back),
    )
    return result, grad_in, down_grad, up_grad


def solution(mesh):
    return jax.shard_map(
        functools.partial(body, mesh.shape["groups"], mesh.shape["dp"]),
        mesh=mesh,
        in_specs=(
            P(("groups", "dp"), None),
            P(("groups", "dp"), None),
            P("dp", None),
            P(None, None, "dp"),
            P(None, "dp"),
            P(),
            P("groups", None),
        ),
        out_specs=(
            P(("groups", "dp"), None),
            P(("groups", "dp"), None),
            P("groups", None, "dp"),
            P("groups", "dp"),
        ),
        check_vma=False,
    )
```

```python
import functools

import jax
import jax.numpy as jnp
from jax import lax
from jax.experimental import pallas as pl
from jax.experimental.pallas import tpu as pltpu
from jax.sharding import PartitionSpec as P

RANK_TILE = 16
AXES = ("groups", "dp")
F32 = jnp.float32
BF16 = jnp.bfloat16
VMEM = pl.BlockSpec(memory_space=pltpu.VMEM)
SMEM = pl.BlockSpec(memory_space=pltpu.SMEM)


def dot(a, b, ca, cb):
    return lax.dot_general(a, b, (((ca,), (cb,)), ((), ())), preferred_element_type=F32)


def call(kernel, outs, scalars, arrays, flops=0):
    size = sum(x.size * x.dtype.itemsize for x in arrays)
    size += sum(x.size * x.dtype.itemsize for x in outs)
    return pl.pallas_call(
        kernel,
        out_shape=outs,
        in_specs=[SMEM] * len(scalars) + [VMEM] * len(arrays),
        out_specs=[VMEM] * len(outs),
        compiler_params=pltpu.CompilerParams(vmem_limit_bytes=60 * 1024 * 1024),
        cost_estimate=pl.CostEstimate(flops=flops, bytes_accessed=size, transcendentals=0),
    )(*scalars, *arrays)


def shape(dims, dtype=BF16):
    return jax.ShapeDtypeStruct(dims, dtype)


def iota(dims, axis):
    return lax.broadcasted_iota(jnp.int32, dims, axis)


def factor_of(ids, ranks, tile, width):
    count = ranks[ids[tile]]
    scale = 2.0 / jnp.full((1, width), count, jnp.int32).astype(F32)
    return jnp.where(iota((1, width), 1) < count * RANK_TILE, scale, 0.0)


def pack_kernel(meta, ids, down, up_own, up_other, blocks):
    adapters, rank, width = down.shape
    chips = blocks.shape[0]
    c = meta[1]
    rows = chips * 16
    q = iota((rows, adapters), 0)
    chosen = jnp.zeros((rows, adapters), jnp.int32)
    for chip in range(chips):
        for slot in range(2):
            adapter = ids[2 * chip + jnp.bitwise_xor(c, slot)]
            blocks[chip, rank * slot : rank * (slot + 1), :] = down[adapter]
            chosen = jnp.where(q // 8 == 2 * chip + slot, adapter, chosen)
    match = chosen == iota((rows, adapters), 1)
    packed = jnp.zeros((rows, width), F32)
    for side, up in enumerate((up_own, up_other)):
        for r in range(4):
            pick = (match & (q % 8 == 4 * side + r)).astype(F32).astype(BF16)
            packed = packed + dot(pick, up[:, width * r : width * (r + 1)], 1, 0)
    packed = packed.astype(BF16)
    for chip in range(chips):
        blocks[chip, 2 * rank : 2 * rank + 16, :] = packed[16 * chip : 16 * (chip + 1), :]


def lane_masks(out_width, width, rank):
    per_row = width // rank
    lane_ok = iota((out_width, width), 1) // rank == iota((out_width, width), 0) % per_row
    fold = (iota((width, rank), 0) % rank == iota((width, rank), 1)).astype(F32).astype(BF16)
    return lane_ok, fold


def rank_kernel(
    meta, ids, ranks, tok_own, tok_sib, og_own, og_sib, blocks, grads, low, back_own, back_sib, up_out
):
    chips, _, width = blocks.shape
    rows = tok_own.shape[0]
    out_width = og_own.shape[1]
    rank = back_own.shape[1]
    k, c = meta[0], meta[1]
    heads = out_width // (2 * chips)
    per_row = width // rank
    packed = jnp.concatenate([blocks[i, 2 * rank : 2 * rank + 16, :] for i in range(chips)], axis=0)
    q = iota((out_width, chips * 16), 1)
    o = iota((out_width, chips * 16), 0)
    device = 2 * (q // 16) + jnp.bitwise_xor(c, (q // 4) % 2)
    place = o // per_row == device * (heads // per_row) + q % 4
    lane_ok, fold = lane_masks(out_width, width, rank)
    for slot, (tok, og, back) in enumerate(
        ((tok_own, og_own, back_own), (tok_sib, og_sib, back_sib))
    ):
        pick = (place & ((q // 8) % 2 == slot)).astype(F32).astype(BF16)
        spread = jnp.where(lane_ok, dot(pick, packed, 1, 0), 0.0).astype(BF16)
        up = dot(spread, fold, 1, 0).astype(BF16)
        if slot == 0:
            up_out[...] = up
        factor = factor_of(ids, ranks, 2 * k + jnp.bitwise_xor(c, slot), rank)
        backward = (dot(og[...], up, 1, 0) * factor).astype(BF16)
        back[...] = backward
        turned = backward.T
        total = jnp.zeros((rows, rank), F32)
        half = slice(rank * slot, rank * (slot + 1))
        for i in range(chips):
            start = pl.multiple_of((2 * i + c) * width, width)
            part = tok[:, pl.ds(start, width)]
            grads[i, half, :] = dot(turned, part, 1, 0).astype(BF16)
            total = total + dot(part, blocks[i, half, :], 1, 1)
        low[rows * slot : rows * (slot + 1), :] = total


def hidden_kernel(chips, meta, ids, ranks, low, other, og_own, og_sib, up, out_low, *terms):
    rows, out_width = og_own.shape
    rank = up.shape[1]
    width = terms[0].shape[1]
    k, c = meta[0], meta[1]
    heads = out_width // (2 * chips)
    per_row = width // rank
    q = iota((chips * 8, out_width), 0)
    o = iota((chips * 8, out_width), 1)
    device = 2 * jnp.bitwise_xor(k, q // 8) + c
    place = o // per_row == device * (heads // per_row) + q % 4
    lane_ok, fold = lane_masks(out_width, width, rank)
    packed = jnp.zeros((chips * 8, width), F32)
    for slot, og in enumerate((og_own, og_sib)):
        factor = factor_of(ids, ranks, 2 * k + jnp.bitwise_xor(c, slot), rank)
        total = low[rows * slot : rows * (slot + 1), :] + other[rows * (1 - slot) : rows * (2 - slot), :]
        hidden = (total * factor).astype(BF16)
        if slot == 0:
            out_low[...] = dot(hidden, up[...], 1, 1)
        term = dot(og[...], hidden, 0, 0).astype(BF16)
        spread = jnp.where(lane_ok, dot(term, fold, 1, 1), 0.0).astype(BF16)
        pick = (place & ((q // 4) % 2 == slot)).astype(F32).astype(BF16)
        packed = packed + dot(pick, spread, 1, 0)
    for j in range(chips):
        terms[j][...] = packed[8 * j : 8 * (j + 1), :].astype(BF16)


def base_kernel(plan, meta, tok_own, tok_sib, og_own, og_sib, back_own, back_sib, blocks, *refs):
    pieces = refs[: len(refs) - 4]
    for_own, for_sib, grad_own, grad_sib = refs[len(refs) - 4 :]
    width = blocks.shape[2]
    rank = back_own.shape[1]
    rows = tok_own.shape[0]
    k, c, g = meta[0], meta[1], meta[2]
    og = jnp.concatenate([og_own[...], og_sib[...]], axis=0)
    total = jnp.zeros((2 * rows, og.shape[1]), F32)
    for index, j, count, side in plan:
        piece = pieces[index]
        chip = jnp.bitwise_xor(k, j)
        shift = 0 if side is None else jnp.bitwise_xor(g, side) * count
        if piece.shape[0] > count:
            weight = piece[pl.ds(pl.multiple_of(chip * count, count), count), :]
        else:
            weight = piece[...]
        start = pl.multiple_of((2 * chip + c) * width + shift, 128)
        tok = jnp.concatenate(
            [tok_own[:, pl.ds(start, count)], tok_sib[:, pl.ds(start, count)]], axis=0
        )
        total = total + dot(tok, weight, 1, 0)
        grad = dot(og, weight, 1, 1)
        inner = pl.ds(pl.multiple_of(shift, 128), count)
        low_own = dot(back_own[...], blocks[chip, 0:rank, inner], 1, 0).astype(BF16)
        low_sib = dot(back_sib[...], blocks[chip, rank : 2 * rank, inner], 1, 0).astype(BF16)
        to = pl.ds(pl.multiple_of(chip * width + shift, 128), count)
        grad_own[:, to] = (grad[:rows] + low_own.astype(F32)).astype(BF16)
        grad_sib[:, to] = (grad[rows:] + low_sib.astype(F32)).astype(BF16)
    for_own[...] = total[:rows]
    for_sib[...] = total[rows:]


def join_kernel(chips, meta, mine, other, out_low, grad_mine, grad_other, result, grad_in):
    c = meta[1]
    result[...] = (mine[...] + other[...] + out_low[...]).astype(BF16)
    width = grad_mine.shape[1] // chips
    for chip in range(chips):
        cols = slice(width * chip, width * (chip + 1))
        own = pl.multiple_of((2 * chip + c) * width, width)
        sib = pl.multiple_of((2 * chip + 1 - c) * width, width)
        grad_in[:, pl.ds(own, width)] = grad_mine[:, cols]
        grad_in[:, pl.ds(sib, width)] = grad_other[:, cols]


def down_kernel(meta, ids, back, out):
    rank = out.shape[1]
    c = meta[1]
    for chip in range(back.shape[0]):
        for slot in range(2):
            adapter = ids[2 * chip + jnp.bitwise_xor(c, slot)]
            out[adapter] = back[chip, rank * slot : rank * (slot + 1), :]


def up_kernel(meta, ids, *refs):
    out, terms = refs[-1], refs[:-1]
    width = terms[0].shape[1]
    k, c = meta[0], meta[1]
    flat = jnp.concatenate([t[...] for t in terms], axis=0)
    q = iota((out.shape[0], flat.shape[0]), 1)
    chosen = jnp.zeros(q.shape, jnp.int32)
    for j in range(len(terms)):
        for slot in range(2):
            adapter = ids[2 * jnp.bitwise_xor(k, j) + jnp.bitwise_xor(c, slot)]
            chosen = jnp.where(q // 4 == 2 * j + slot, adapter, chosen)
    match = chosen == iota(q.shape, 0)
    for r in range(4):
        pick = (match & (q % 4 == r)).astype(F32).astype(BF16)
        out[:, width * r : width * (r + 1)] = dot(pick, flat, 1, 0).astype(BF16)


def pairs(groups, size, to):
    out = []
    for g in range(groups):
        for d in range(size):
            target = to(g, d)
            if target is not None:
                out.append((g * size + d, target[0] * size + target[1]))
    return out


def gather_weight(weight, groups, size, send):
    chips = size // 2
    rows = weight.shape[0]
    if groups != 2 or chips != 8:
        lists = [[2 * chip + core for chip in range(chips)] for core in range(2)]
        full = lax.all_gather(weight, "dp", axis=0, tiled=True, axis_index_groups=lists)
        return [full], [(0, j, rows, None) for j in range(chips)]
    half = rows // 2
    place = lax.axis_index("dp")
    z = place // 4
    middle = (z == 1) | (z == 2)
    mine = lax.dynamic_slice_in_dim(weight, lax.axis_index("groups") * half, half)
    swap_x = lambda g, d: (1 - g, d)
    swap_y = lambda g, d: (g, d ^ 2)
    swap_near = lambda g, d: (g, d ^ 4)
    swap_mid = lambda g, d: (g, d ^ 12) if d // 4 in (1, 2) else None
    outward = lambda g, d: (g, d ^ 4) if d // 4 in (1, 2) else None
    near = send(mine, swap_near)
    cross = send(mine, swap_mid)
    own_y = send(weight, swap_y)
    cross_near = send(near, swap_mid)
    edge = send(cross, outward)
    edge_near = send(cross_near, outward)
    by_slot = (
        (2, near),
        (4, jnp.where(middle, cross_near, edge)),
        (6, jnp.where(middle, cross, edge_near)),
    )
    arrays = [weight, own_y]
    plan = [(0, 0, rows, None), (1, 1, rows, None)]
    for j, held in by_slot:
        over_y = send(held, swap_y)
        first = len(arrays)
        arrays += [held, send(held, swap_x), over_y, send(over_y, swap_x)]
        plan += [(first + i, j + i // 2, half, i % 2) for i in range(4)]
    return arrays, plan


def body(groups, size, tokens, out_grad, base_weight, adapter_down, adapter_up, rank_tiles, tile_adapter):
    chips = size // 2
    rows, model_width = tokens.shape
    out_width = out_grad.shape[1]
    adapters, rank, width = adapter_down.shape
    ids = tile_adapter[:, 0]
    place = lax.axis_index("dp")
    meta = jnp.stack([place // 2, place % 2, lax.axis_index("groups")]).astype(jnp.int32)

    def send(x, to):
        return lax.ppermute(x, AXES, pairs(groups, size, to))

    def sibling(x):
        return send(x, lambda g, d: (g, d ^ 1))

    same_core = [[2 * chip + core for chip in range(chips)] for core in range(2)]

    def exchange(blocks):
        return lax.all_to_all(
            blocks, "dp", split_axis=0, concat_axis=0, tiled=True, axis_index_groups=same_core
        )

    up_sib = sibling(adapter_up)
    tok_sib = sibling(tokens)
    og_sib = sibling(out_grad)
    (packed,) = call(
        pack_kernel,
        [shape((chips, 2 * rank + 16, width))],
        (meta, ids),
        (adapter_down, adapter_up, up_sib),
    )
    blocks = exchange(packed)
    weights, plan = gather_weight(base_weight, groups, size, send)

    grads, low, back_own, back_sib, up_mine = call(
        rank_kernel,
        [
            shape((chips, 2 * rank, width)),
            shape((2 * rows, rank), F32),
            shape((rows, rank)),
            shape((rows, rank)),
            shape((out_width, rank)),
        ],
        (meta, ids, rank_tiles),
        (tokens, tok_sib, out_grad, og_sib, blocks),
        flops=4 * rows * model_width * rank,
    )
    grads_back = exchange(grads)
    out_low, *terms = call(
        functools.partial(hidden_kernel, chips),
        [shape((rows, out_width), F32)] + [shape((8, width))] * chips,
        (meta, ids, rank_tiles),
        (low, sibling(low), out_grad, og_sib, up_mine),
        flops=4 * rows * out_width * rank,
    )
    terms_back = terms[:1] + [
        send(terms[j], lambda g, d: (g, d ^ (2 * j))) for j in range(1, chips)
    ]
    (up_grad,) = call(up_kernel, [shape(adapter_up.shape)], (meta, ids), tuple(terms_back))

    for_own, for_sib, grad_own, grad_sib = call(
        functools.partial(base_kernel, plan),
        [shape((rows, out_width), F32)] * 2 + [shape((rows, model_width // 2))] * 2,
        (meta,),
        (tokens, tok_sib, out_grad, og_sib, back_own, back_sib, blocks, *weights),
        flops=4 * rows * model_width * out_width,
    )
    for_other, grad_other = sibling(for_sib), sibling(grad_sib)
    result, grad_in = call(
        functools.partial(join_kernel, chips),
        [shape((rows, out_width)), shape((rows, model_width))],
        (meta,),
        (for_own, for_other, out_low, grad_own, grad_other),
    )
    (down_grad,) = call(
        down_kernel,
        [shape(adapter_down.shape)],
        (meta, ids),
        (grads_back,),
    )
    return result, grad_in, down_grad, up_grad


def solution(mesh):
    return jax.shard_map(
        functools.partial(body, mesh.shape["groups"], mesh.shape["dp"]),
        mesh=mesh,
        in_specs=(
            P(("groups", "dp"), None),
            P(("groups", "dp"), None),
            P("dp", None),
            P(None, None, "dp"),
            P(None, "dp"),
            P(),
            P("groups", None),
        ),
        out_specs=(
            P(("groups", "dp"), None),
            P(("groups", "dp"), None),
            P("groups", None, "dp"),
            P("groups", "dp"),
        ),
        check_vma=False,
    )
```

```python
import functools

import jax
import jax.numpy as jnp
from jax import lax
from jax.experimental import pallas as pl
from jax.experimental.pallas import tpu as pltpu
from jax.sharding import PartitionSpec as P

RANK_TILE = 16
AXES = ("groups", "dp")
F32 = jnp.float32
BF16 = jnp.bfloat16
VMEM = pl.BlockSpec(memory_space=pltpu.VMEM)
SMEM = pl.BlockSpec(memory_space=pltpu.SMEM)


def dot(a, b, ca, cb):
    return lax.dot_general(a, b, (((ca,), (cb,)), ((), ())), preferred_element_type=F32)


def call(kernel, outs, scalars, arrays, flops=0):
    size = sum(x.size * x.dtype.itemsize for x in arrays)
    size += sum(x.size * x.dtype.itemsize for x in outs)
    return pl.pallas_call(
        kernel,
        out_shape=outs,
        in_specs=[SMEM] * len(scalars) + [VMEM] * len(arrays),
        out_specs=[VMEM] * len(outs),
        compiler_params=pltpu.CompilerParams(vmem_limit_bytes=60 * 1024 * 1024),
        cost_estimate=pl.CostEstimate(flops=flops, bytes_accessed=size, transcendentals=0),
    )(*scalars, *arrays)


def shape(dims, dtype=BF16):
    return jax.ShapeDtypeStruct(dims, dtype)


def iota(dims, axis):
    return lax.broadcasted_iota(jnp.int32, dims, axis)


def factor_of(ids, ranks, tile, width):
    count = ranks[ids[tile]]
    scale = 2.0 / jnp.full((1, width), count, jnp.int32).astype(F32)
    return jnp.where(iota((1, width), 1) < count * RANK_TILE, scale, 0.0)


def pack_kernel(meta, ids, down, up_own, up_other, blocks):
    adapters, rank, width = down.shape
    chips = blocks.shape[0]
    c = meta[1]
    rows = chips * 16
    q = iota((rows, adapters), 0)
    chosen = jnp.zeros((rows, adapters), jnp.int32)
    for chip in range(chips):
        for slot in range(2):
            adapter = ids[2 * chip + jnp.bitwise_xor(c, slot)]
            blocks[chip, rank * slot : rank * (slot + 1), :] = down[adapter]
            chosen = jnp.where(q // 8 == 2 * chip + slot, adapter, chosen)
    match = chosen == iota((rows, adapters), 1)
    packed = jnp.zeros((rows, width), F32)
    for side, up in enumerate((up_own, up_other)):
        for r in range(4):
            pick = (match & (q % 8 == 4 * side + r)).astype(F32).astype(BF16)
            packed = packed + dot(pick, up[:, width * r : width * (r + 1)], 1, 0)
    packed = packed.astype(BF16)
    for chip in range(chips):
        blocks[chip, 2 * rank : 2 * rank + 16, :] = packed[16 * chip : 16 * (chip + 1), :]


def lane_masks(out_width, width, rank):
    per_row = width // rank
    lane_ok = iota((out_width, width), 1) // rank == iota((out_width, width), 0) % per_row
    fold = (iota((width, rank), 0) % rank == iota((width, rank), 1)).astype(F32).astype(BF16)
    return lane_ok, fold


def rank_kernel(
    meta, ids, ranks, tok_own, tok_sib, og_own, og_sib, blocks, grads, low, back_own, back_sib, up_out
):
    chips, _, width = blocks.shape
    rows = tok_own.shape[0]
    out_width = og_own.shape[1]
    rank = back_own.shape[1]
    k, c = meta[0], meta[1]
    heads = out_width // (2 * chips)
    per_row = width // rank
    packed = jnp.concatenate([blocks[i, 2 * rank : 2 * rank + 16, :] for i in range(chips)], axis=0)
    q = iota((out_width, chips * 16), 1)
    o = iota((out_width, chips * 16), 0)
    device = 2 * (q // 16) + jnp.bitwise_xor(c, (q // 4) % 2)
    place = o // per_row == device * (heads // per_row) + q % 4
    lane_ok, fold = lane_masks(out_width, width, rank)
    for slot, (tok, og, back) in enumerate(
        ((tok_own, og_own, back_own), (tok_sib, og_sib, back_sib))
    ):
        pick = (place & ((q // 8) % 2 == slot)).astype(F32).astype(BF16)
        spread = jnp.where(lane_ok, dot(pick, packed, 1, 0), 0.0).astype(BF16)
        up = dot(spread, fold, 1, 0).astype(BF16)
        if slot == 0:
            up_out[...] = up
        factor = factor_of(ids, ranks, 2 * k + jnp.bitwise_xor(c, slot), rank)
        backward = (dot(og[...], up, 1, 0) * factor).astype(BF16)
        back[...] = backward
        turned = backward.T
        total = jnp.zeros((rows, rank), F32)
        half = slice(rank * slot, rank * (slot + 1))
        for i in range(chips):
            start = pl.multiple_of((2 * i + c) * width, width)
            part = tok[:, pl.ds(start, width)]
            grads[i, half, :] = dot(turned, part, 1, 0).astype(BF16)
            total = total + dot(part, blocks[i, half, :], 1, 1)
        low[rows * slot : rows * (slot + 1), :] = total


def hidden_kernel(meta, ids, ranks, low, other, og_own, og_sib, up, grads, out_low, terms):
    chips, _, width = terms.shape
    rows, out_width = og_own.shape
    rank = up.shape[1]
    k, c = meta[0], meta[1]
    heads = out_width // (2 * chips)
    per_row = width // rank
    q = iota((chips * 16, out_width), 0)
    o = iota((chips * 16, out_width), 1)
    place = o // per_row == (2 * (q // 16) + c) * (heads // per_row) + q % 4
    lane_ok, fold = lane_masks(out_width, width, rank)
    packed = jnp.zeros((chips * 16, width), F32)
    for slot, og in enumerate((og_own, og_sib)):
        factor = factor_of(ids, ranks, 2 * k + jnp.bitwise_xor(c, slot), rank)
        total = low[rows * slot : rows * (slot + 1), :] + other[rows * (1 - slot) : rows * (2 - slot), :]
        hidden = (total * factor).astype(BF16)
        if slot == 0:
            out_low[...] = dot(hidden, up[...], 1, 1)
        term = dot(og[...], hidden, 0, 0).astype(BF16)
        spread = jnp.where(lane_ok, dot(term, fold, 1, 1), 0.0).astype(BF16)
        pick = (place & ((q // 4) % 4 == slot)).astype(F32).astype(BF16)
        packed = packed + dot(pick, spread, 1, 0)
    terms[...] = packed.astype(BF16).reshape(terms.shape)


def base_kernel(plan, meta, tok_own, tok_sib, og_own, og_sib, back_own, back_sib, blocks, *refs):
    pieces = refs[: len(refs) - 4]
    for_own, for_sib, grad_own, grad_sib = refs[len(refs) - 4 :]
    width = blocks.shape[2]
    rank = back_own.shape[1]
    rows = tok_own.shape[0]
    k, c, g = meta[0], meta[1], meta[2]
    og = jnp.concatenate([og_own[...], og_sib[...]], axis=0)
    total = jnp.zeros((2 * rows, og.shape[1]), F32)
    for index, j, count, side in plan:
        piece = pieces[index]
        chip = jnp.bitwise_xor(k, j)
        shift = 0 if side is None else jnp.bitwise_xor(g, side) * count
        if piece.shape[0] > count:
            weight = piece[pl.ds(pl.multiple_of(chip * count, count), count), :]
        else:
            weight = piece[...]
        start = pl.multiple_of((2 * chip + c) * width + shift, 128)
        tok = jnp.concatenate(
            [tok_own[:, pl.ds(start, count)], tok_sib[:, pl.ds(start, count)]], axis=0
        )
        total = total + dot(tok, weight, 1, 0)
        grad = dot(og, weight, 1, 1)
        inner = pl.ds(pl.multiple_of(shift, 128), count)
        low_own = dot(back_own[...], blocks[chip, 0:rank, inner], 1, 0).astype(BF16)
        low_sib = dot(back_sib[...], blocks[chip, rank : 2 * rank, inner], 1, 0).astype(BF16)
        to = pl.ds(pl.multiple_of(chip * width + shift, 128), count)
        grad_own[:, to] = (grad[:rows] + low_own.astype(F32)).astype(BF16)
        grad_sib[:, to] = (grad[rows:] + low_sib.astype(F32)).astype(BF16)
    for_own[...] = total[:rows]
    for_sib[...] = total[rows:]


def join_kernel(chips, meta, mine, other, out_low, grad_mine, grad_other, result, grad_in):
    c = meta[1]
    result[...] = (mine[...] + other[...] + out_low[...]).astype(BF16)
    width = grad_mine.shape[1] // chips
    for chip in range(chips):
        cols = slice(width * chip, width * (chip + 1))
        own = pl.multiple_of((2 * chip + c) * width, width)
        sib = pl.multiple_of((2 * chip + 1 - c) * width, width)
        grad_in[:, pl.ds(own, width)] = grad_mine[:, cols]
        grad_in[:, pl.ds(sib, width)] = grad_other[:, cols]


def back_kernel(meta, ids, back, down_out, up_out):
    rank = down_out.shape[1]
    chips, _, width = back.shape
    c = meta[1]
    flat = jnp.concatenate([back[i, 2 * rank : 2 * rank + 16, :] for i in range(chips)], axis=0)
    q = iota((up_out.shape[0], chips * 16), 1)
    chosen = jnp.full(q.shape, -1, jnp.int32)
    for chip in range(chips):
        for slot in range(2):
            adapter = ids[2 * chip + jnp.bitwise_xor(c, slot)]
            down_out[adapter] = back[chip, rank * slot : rank * (slot + 1), :]
            chosen = jnp.where(q // 4 == 4 * chip + slot, adapter, chosen)
    match = chosen == iota(q.shape, 0)
    for r in range(4):
        pick = (match & (q % 4 == r)).astype(F32).astype(BF16)
        up_out[:, width * r : width * (r + 1)] = dot(pick, flat, 1, 0).astype(BF16)


def after(x, *others):
    return lax.optimization_barrier((x, *others))[0]


def pairs(groups, size, to):
    out = []
    for g in range(groups):
        for d in range(size):
            target = to(g, d)
            if target is not None:
                out.append((g * size + d, target[0] * size + target[1]))
    return out


def gather_weight(weight, groups, size, send):
    chips = size // 2
    rows = weight.shape[0]
    if groups != 2 or chips != 8:
        lists = [[2 * chip + core for chip in range(chips)] for core in range(2)]
        full = lax.all_gather(weight, "dp", axis=0, tiled=True, axis_index_groups=lists)
        return [full], [(0, j, rows, None) for j in range(chips)], (), ()
    half = rows // 2
    mine = lax.dynamic_slice_in_dim(weight, lax.axis_index("groups") * half, half)
    swap_x = lambda g, d: (1 - g, d)
    swap_y = lambda g, d: (g, d ^ 2)
    far = send(mine, lambda g, d: (g, d ^ 12))
    near = send(mine, lambda g, d: (g, d ^ 4))
    own_y = send(weight, swap_y)
    far_near = send(far, lambda g, d: (g, d ^ 4))
    arrays = [weight, own_y]
    plan = [(0, 0, rows, None), (1, 1, rows, None)]
    for j, held in ((2, near), (6, far), (4, far_near)):
        over_y = send(held, swap_y)
        first = len(arrays)
        arrays += [held, send(held, swap_x), over_y, send(over_y, swap_x)]
        plan += [(first + i, j + i // 2, half, i % 2) for i in range(4)]
    return arrays, plan, (own_y, near, far_near), arrays[:-1]


def body(groups, size, tokens, out_grad, base_weight, adapter_down, adapter_up, rank_tiles, tile_adapter):
    chips = size // 2
    rows, model_width = tokens.shape
    out_width = out_grad.shape[1]
    adapters, rank, width = adapter_down.shape
    ids = tile_adapter[:, 0]
    place = lax.axis_index("dp")
    meta = jnp.stack([place // 2, place % 2, lax.axis_index("groups")]).astype(jnp.int32)

    def send(x, to):
        return lax.ppermute(x, AXES, pairs(groups, size, to))

    def sibling(x):
        return send(x, lambda g, d: (g, d ^ 1))

    same_core = [[2 * chip + core for chip in range(chips)] for core in range(2)]

    def exchange(blocks):
        return lax.all_to_all(
            blocks, "dp", split_axis=0, concat_axis=0, tiled=True, axis_index_groups=same_core
        )

    up_sib = sibling(adapter_up)
    tok_sib = sibling(tokens)
    og_sib = sibling(out_grad)
    (packed,) = call(
        pack_kernel,
        [shape((chips, 2 * rank + 16, width))],
        (meta, ids),
        (adapter_down, adapter_up, up_sib),
    )
    weights, plan, first, early = gather_weight(base_weight, groups, size, send)
    blocks = exchange(after(packed, *first))

    grads, low, back_own, back_sib, up_mine = call(
        rank_kernel,
        [
            shape((chips, 2 * rank + 16, width)),
            shape((2 * rows, rank), F32),
            shape((rows, rank)),
            shape((rows, rank)),
            shape((out_width, rank)),
        ],
        (meta, ids, rank_tiles),
        (tokens, tok_sib, out_grad, og_sib, blocks),
        flops=4 * rows * model_width * rank,
    )
    size_up = pl.BlockSpec((chips, 16, width), lambda i: (0, rank // 8, 0))
    out_low, grads = pl.pallas_call(
        hidden_kernel,
        grid=(1,),
        out_shape=[shape((rows, out_width), F32), shape(grads.shape)],
        in_specs=[SMEM] * 3 + [VMEM] * 5 + [pl.BlockSpec(memory_space=pl.ANY)],
        out_specs=[pl.BlockSpec((rows, out_width), lambda i: (0, 0)), size_up],
        input_output_aliases={8: 1},
        compiler_params=pltpu.CompilerParams(vmem_limit_bytes=60 * 1024 * 1024),
    )(meta, ids, rank_tiles, low, sibling(low), after(out_grad, *early), og_sib, up_mine, grads)
    grads_back = exchange(grads)

    for_own, for_sib, grad_own, grad_sib = call(
        functools.partial(base_kernel, plan),
        [shape((rows, out_width), F32)] * 2 + [shape((rows, model_width // 2))] * 2,
        (meta,),
        (tokens, tok_sib, out_grad, og_sib, after(back_own, out_low), back_sib, blocks, *weights),
        flops=4 * rows * model_width * out_width,
    )
    for_other, grad_other = sibling(for_sib), sibling(grad_sib)
    result, grad_in = call(
        functools.partial(join_kernel, chips),
        [shape((rows, out_width)), shape((rows, model_width))],
        (meta,),
        (for_own, for_other, out_low, grad_own, grad_other),
    )
    down_grad, up_grad = call(
        back_kernel,
        [shape(adapter_down.shape), shape(adapter_up.shape)],
        (meta, ids),
        (grads_back,),
    )
    return result, grad_in, down_grad, up_grad


def solution(mesh):
    return jax.shard_map(
        functools.partial(body, mesh.shape["groups"], mesh.shape["dp"]),
        mesh=mesh,
        in_specs=(
            P(("groups", "dp"), None),
            P(("groups", "dp"), None),
            P("dp", None),
            P(None, None, "dp"),
            P(None, "dp"),
            P(),
            P("groups", None),
        ),
        out_specs=(
            P(("groups", "dp"), None),
            P(("groups", "dp"), None),
            P("groups", None, "dp"),
            P("groups", "dp"),
        ),
        check_vma=False,
    )
```

```python
import functools

import jax
import jax.numpy as jnp
from jax import lax
from jax.experimental import pallas as pl
from jax.experimental.pallas import tpu as pltpu
from jax.sharding import PartitionSpec as P

RANK_TILE = 16
AXES = ("groups", "dp")
F32 = jnp.float32
BF16 = jnp.bfloat16
VMEM = pl.BlockSpec(memory_space=pltpu.VMEM)
SMEM = pl.BlockSpec(memory_space=pltpu.SMEM)


def dot(a, b, ca, cb):
    return lax.dot_general(a, b, (((ca,), (cb,)), ((), ())), preferred_element_type=F32)


def call(kernel, outs, scalars, arrays, flops=0):
    size = sum(x.size * x.dtype.itemsize for x in arrays)
    size += sum(x.size * x.dtype.itemsize for x in outs)
    return pl.pallas_call(
        kernel,
        out_shape=outs,
        in_specs=[SMEM] * len(scalars) + [VMEM] * len(arrays),
        out_specs=[VMEM] * len(outs),
        compiler_params=pltpu.CompilerParams(vmem_limit_bytes=30 * 1024 * 1024),
        cost_estimate=pl.CostEstimate(flops=flops, bytes_accessed=size, transcendentals=0),
    )(*scalars, *arrays)


def shape(dims, dtype=BF16):
    return jax.ShapeDtypeStruct(dims, dtype)


def iota(dims, axis):
    return lax.broadcasted_iota(jnp.int32, dims, axis)


def factor_of(ids, ranks, tile, width):
    count = ranks[ids[tile]]
    scale = 2.0 / jnp.full((1, width), count, jnp.int32).astype(F32)
    return jnp.where(iota((1, width), 1) < count * RANK_TILE, scale, 0.0)


def pack_kernel(meta, ids, down, up_own, up_other, blocks):
    adapters, rank, width = down.shape
    chips = blocks.shape[0]
    c = meta[1]
    rows = chips * 16
    q = iota((rows, adapters), 0)
    chosen = jnp.zeros((rows, adapters), jnp.int32)
    for chip in range(chips):
        for slot in range(2):
            adapter = ids[2 * chip + jnp.bitwise_xor(c, slot)]
            blocks[chip, rank * slot : rank * (slot + 1), :] = down[adapter]
            chosen = jnp.where(q // 8 == 2 * chip + slot, adapter, chosen)
    match = chosen == iota((rows, adapters), 1)
    packed = jnp.zeros((rows, width), F32)
    for side, up in enumerate((up_own, up_other)):
        for r in range(4):
            pick = (match & (q % 8 == 4 * side + r)).astype(F32).astype(BF16)
            packed = packed + dot(pick, up[:, width * r : width * (r + 1)], 1, 0)
    packed = packed.astype(BF16)
    for chip in range(chips):
        blocks[chip, 2 * rank : 2 * rank + 16, :] = packed[16 * chip : 16 * (chip + 1), :]


def lane_masks(out_width, width, rank):
    per_row = width // rank
    lane_ok = iota((out_width, width), 1) // rank == iota((out_width, width), 0) % per_row
    fold = (iota((width, rank), 0) % rank == iota((width, rank), 1)).astype(F32).astype(BF16)
    return lane_ok, fold


def rank_kernel(
    meta, ids, ranks, tok_own, tok_sib, og_own, og_sib, blocks, grads, low, back_own, back_sib, up_out
):
    chips, _, width = blocks.shape
    rows = tok_own.shape[0]
    out_width = og_own.shape[1]
    rank = back_own.shape[1]
    k, c = meta[0], meta[1]
    heads = out_width // (2 * chips)
    per_row = width // rank
    packed = jnp.concatenate([blocks[i, 2 * rank : 2 * rank + 16, :] for i in range(chips)], axis=0)
    q = iota((out_width, chips * 16), 1)
    o = iota((out_width, chips * 16), 0)
    device = 2 * (q // 16) + jnp.bitwise_xor(c, (q // 4) % 2)
    place = o // per_row == device * (heads // per_row) + q % 4
    lane_ok, fold = lane_masks(out_width, width, rank)
    for slot, (tok, og, back) in enumerate(
        ((tok_own, og_own, back_own), (tok_sib, og_sib, back_sib))
    ):
        pick = (place & ((q // 8) % 2 == slot)).astype(F32).astype(BF16)
        spread = jnp.where(lane_ok, dot(pick, packed, 1, 0), 0.0).astype(BF16)
        up = dot(spread, fold, 1, 0).astype(BF16)
        if slot == 0:
            up_out[...] = up
        factor = factor_of(ids, ranks, 2 * k + jnp.bitwise_xor(c, slot), rank)
        backward = (dot(og[...], up, 1, 0) * factor).astype(BF16)
        back[...] = backward
        turned = backward.T
        total = jnp.zeros((rows, rank), F32)
        half = slice(rank * slot, rank * (slot + 1))
        for i in range(chips):
            start = pl.multiple_of((2 * i + c) * width, width)
            part = tok[:, pl.ds(start, width)]
            grads[i, half, :] = dot(turned, part, 1, 0).astype(BF16)
            total = total + dot(part, blocks[i, half, :], 1, 1)
        low[rows * slot : rows * (slot + 1), :] = total


def hidden_kernel(meta, ids, ranks, low, other, og_own, og_sib, up, grads, out_low, terms):
    chips, _, width = terms.shape
    rows, out_width = og_own.shape
    rank = up.shape[1]
    k, c = meta[0], meta[1]
    heads = out_width // (2 * chips)
    per_row = width // rank
    q = iota((chips * 16, out_width), 0)
    o = iota((chips * 16, out_width), 1)
    place = o // per_row == (2 * (q // 16) + c) * (heads // per_row) + q % 4
    lane_ok, fold = lane_masks(out_width, width, rank)
    packed = jnp.zeros((chips * 16, width), F32)
    for slot, og in enumerate((og_own, og_sib)):
        factor = factor_of(ids, ranks, 2 * k + jnp.bitwise_xor(c, slot), rank)
        total = low[rows * slot : rows * (slot + 1), :] + other[rows * (1 - slot) : rows * (2 - slot), :]
        hidden = (total * factor).astype(BF16)
        if slot == 0:
            out_low[...] = dot(hidden, up[...], 1, 1)
        term = dot(og[...], hidden, 0, 0).astype(BF16)
        spread = jnp.where(lane_ok, dot(term, fold, 1, 1), 0.0).astype(BF16)
        pick = (place & ((q // 4) % 4 == slot)).astype(F32).astype(BF16)
        packed = packed + dot(pick, spread, 1, 0)
    terms[...] = packed.astype(BF16).reshape(terms.shape)


def base_kernel(plan, meta, tok_own, tok_sib, og_own, og_sib, back_own, back_sib, blocks, *refs):
    pieces = refs[: len(refs) - 4]
    for_own, for_sib, grad_own, grad_sib = refs[len(refs) - 4 :]
    width = blocks.shape[2]
    rank = back_own.shape[1]
    rows = tok_own.shape[0]
    k, c, g = meta[0], meta[1], meta[2]
    og = jnp.concatenate([og_own[...], og_sib[...]], axis=0)
    total = jnp.zeros((2 * rows, og.shape[1]), F32)
    for index, j, count, side in plan:
        piece = pieces[index]
        chip = jnp.bitwise_xor(k, j)
        shift = 0 if side is None else jnp.bitwise_xor(g, side) * count
        if piece.shape[0] > count:
            weight = piece[pl.ds(pl.multiple_of(chip * count, count), count), :]
        else:
            weight = piece[...]
        start = pl.multiple_of((2 * chip + c) * width + shift, 128)
        tok = jnp.concatenate(
            [tok_own[:, pl.ds(start, count)], tok_sib[:, pl.ds(start, count)]], axis=0
        )
        total = total + dot(tok, weight, 1, 0)
        grad = dot(og, weight, 1, 1)
        inner = pl.ds(pl.multiple_of(shift, 128), count)
        low_own = dot(back_own[...], blocks[chip, 0:rank, inner], 1, 0).astype(BF16)
        low_sib = dot(back_sib[...], blocks[chip, rank : 2 * rank, inner], 1, 0).astype(BF16)
        to = pl.ds(pl.multiple_of(chip * width + shift, 128), count)
        grad_own[:, to] = (grad[:rows] + low_own.astype(F32)).astype(BF16)
        grad_sib[:, to] = (grad[rows:] + low_sib.astype(F32)).astype(BF16)
    for_own[...] = total[:rows]
    for_sib[...] = total[rows:]


def join_kernel(chips, meta, mine, other, out_low, grad_mine, grad_other, result, grad_in):
    c = meta[1]
    result[...] = (mine[...] + other[...] + out_low[...]).astype(BF16)
    width = grad_mine.shape[1] // chips
    for chip in range(chips):
        cols = slice(width * chip, width * (chip + 1))
        own = pl.multiple_of((2 * chip + c) * width, width)
        sib = pl.multiple_of((2 * chip + 1 - c) * width, width)
        grad_in[:, pl.ds(own, width)] = grad_mine[:, cols]
        grad_in[:, pl.ds(sib, width)] = grad_other[:, cols]


def back_kernel(meta, ids, back, down_out, up_out):
    rank = down_out.shape[1]
    chips, _, width = back.shape
    c = meta[1]
    flat = jnp.concatenate([back[i, 2 * rank : 2 * rank + 16, :] for i in range(chips)], axis=0)
    q = iota((up_out.shape[0], chips * 16), 1)
    chosen = jnp.full(q.shape, -1, jnp.int32)
    for chip in range(chips):
        for slot in range(2):
            adapter = ids[2 * chip + jnp.bitwise_xor(c, slot)]
            down_out[adapter] = back[chip, rank * slot : rank * (slot + 1), :]
            chosen = jnp.where(q // 4 == 4 * chip + slot, adapter, chosen)
    match = chosen == iota(q.shape, 0)
    for r in range(4):
        pick = (match & (q % 4 == r)).astype(F32).astype(BF16)
        up_out[:, width * r : width * (r + 1)] = dot(pick, flat, 1, 0).astype(BF16)


def after(x, *others):
    return lax.optimization_barrier((x, *others))[0]


def pairs(groups, size, to):
    out = []
    for g in range(groups):
        for d in range(size):
            target = to(g, d)
            if target is not None:
                out.append((g * size + d, target[0] * size + target[1]))
    return out


def gather_weight(weight, groups, size, send, packed):
    chips = size // 2
    rows = weight.shape[0]
    if groups != 2 or chips != 8:
        lists = [[2 * chip + core for chip in range(chips)] for core in range(2)]
        full = lax.all_gather(weight, "dp", axis=0, tiled=True, axis_index_groups=lists)
        return [full], [(0, j, rows, None) for j in range(chips)], (), ()
    half = rows // 2
    mine = lax.dynamic_slice_in_dim(weight, lax.axis_index("groups") * half, half)
    swap_x = lambda g, d: (1 - g, d)
    swap_y = lambda g, d: (g, d ^ 2)
    far = send(mine, lambda g, d: (g, d ^ 12))
    near = send(mine, lambda g, d: (g, d ^ 4))
    own_y = send(weight, swap_y)
    far_near = send(after(far, packed), lambda g, d: (g, d ^ 4))
    arrays = [weight, own_y]
    plan = [(0, 0, rows, None), (1, 1, rows, None)]
    for j, held in ((2, near), (6, far), (4, far_near)):
        over_y = send(held, swap_y)
        first = len(arrays)
        arrays += [held, send(held, swap_x), over_y, send(over_y, swap_x)]
        plan += [(first + i, j + i // 2, half, i % 2) for i in range(4)]
    return arrays, plan, (own_y, near, far), arrays[:-1]


def body(groups, size, tokens, out_grad, base_weight, adapter_down, adapter_up, rank_tiles, tile_adapter):
    chips = size // 2
    rows, model_width = tokens.shape
    out_width = out_grad.shape[1]
    adapters, rank, width = adapter_down.shape
    ids = tile_adapter[:, 0]
    place = lax.axis_index("dp")
    meta = jnp.stack([place // 2, place % 2, lax.axis_index("groups")]).astype(jnp.int32)

    def send(x, to):
        return lax.ppermute(x, AXES, pairs(groups, size, to))

    def sibling(x):
        return send(x, lambda g, d: (g, d ^ 1))

    same_core = [[2 * chip + core for chip in range(chips)] for core in range(2)]

    def exchange(blocks):
        return lax.all_to_all(
            blocks, "dp", split_axis=0, concat_axis=0, tiled=True, axis_index_groups=same_core
        )

    up_sib = sibling(adapter_up)
    tok_sib = sibling(tokens)
    og_sib = sibling(out_grad)
    (packed,) = call(
        pack_kernel,
        [shape((chips, 2 * rank + 16, width))],
        (meta, ids),
        (adapter_down, adapter_up, up_sib),
    )
    weights, plan, first, early = gather_weight(base_weight, groups, size, send, packed)
    blocks = exchange(after(packed, tok_sib, og_sib, *first))

    grads, low, back_own, back_sib, up_mine = call(
        rank_kernel,
        [
            shape((chips, 2 * rank + 16, width)),
            shape((2 * rows, rank), F32),
            shape((rows, rank)),
            shape((rows, rank)),
            shape((out_width, rank)),
        ],
        (meta, ids, rank_tiles),
        (tokens, tok_sib, out_grad, og_sib, blocks),
        flops=4 * rows * model_width * rank,
    )
    size_up = pl.BlockSpec((chips, 16, width), lambda i: (0, rank // 8, 0))
    out_low, grads = pl.pallas_call(
        hidden_kernel,
        grid=(1,),
        out_shape=[shape((rows, out_width), F32), shape(grads.shape)],
        in_specs=[SMEM] * 3 + [VMEM] * 5 + [pl.BlockSpec(memory_space=pl.ANY)],
        out_specs=[pl.BlockSpec((rows, out_width), lambda i: (0, 0)), size_up],
        input_output_aliases={8: 1},
        compiler_params=pltpu.CompilerParams(vmem_limit_bytes=30 * 1024 * 1024),
    )(meta, ids, rank_tiles, low, sibling(low), after(out_grad, *early), og_sib, up_mine, grads)
    grads_back = exchange(grads)

    for_own, for_sib, grad_own, grad_sib = call(
        functools.partial(base_kernel, plan),
        [shape((rows, out_width), F32)] * 2 + [shape((rows, model_width // 2))] * 2,
        (meta,),
        (tokens, tok_sib, out_grad, og_sib, after(back_own, out_low), back_sib, blocks, *weights),
        flops=4 * rows * model_width * out_width,
    )
    for_other, grad_other = sibling(for_sib), sibling(grad_sib)
    result, grad_in = call(
        functools.partial(join_kernel, chips),
        [shape((rows, out_width)), shape((rows, model_width))],
        (meta,),
        (for_own, for_other, out_low, grad_own, grad_other),
    )
    down_grad, up_grad = call(
        back_kernel,
        [shape(adapter_down.shape), shape(adapter_up.shape)],
        (meta, ids),
        (grads_back,),
    )
    return result, grad_in, down_grad, up_grad


def solution(mesh):
    return jax.shard_map(
        functools.partial(body, mesh.shape["groups"], mesh.shape["dp"]),
        mesh=mesh,
        in_specs=(
            P(("groups", "dp"), None),
            P(("groups", "dp"), None),
            P("dp", None),
            P(None, None, "dp"),
            P(None, "dp"),
            P(),
            P("groups", None),
        ),
        out_specs=(
            P(("groups", "dp"), None),
            P(("groups", "dp"), None),
            P("groups", None, "dp"),
            P("groups", "dp"),
        ),
        check_vma=False,
    )
```

```python
import functools

import jax
import jax.numpy as jnp
from jax import lax
from jax.experimental import pallas as pl
from jax.experimental.pallas import tpu as pltpu
from jax.sharding import PartitionSpec as P

RANK_TILE = 16
AXES = ("groups", "dp")
F32 = jnp.float32
BF16 = jnp.bfloat16
VMEM = pl.BlockSpec(memory_space=pltpu.VMEM)
SMEM = pl.BlockSpec(memory_space=pltpu.SMEM)


def dot(a, b, ca, cb):
    return lax.dot_general(a, b, (((ca,), (cb,)), ((), ())), preferred_element_type=F32)


def call(kernel, outs, scalars, arrays, flops=0, room=30):
    size = sum(x.size * x.dtype.itemsize for x in arrays)
    size += sum(x.size * x.dtype.itemsize for x in outs)
    return pl.pallas_call(
        kernel,
        out_shape=outs,
        in_specs=[SMEM] * len(scalars) + [VMEM] * len(arrays),
        out_specs=[VMEM] * len(outs),
        compiler_params=pltpu.CompilerParams(vmem_limit_bytes=room * 1024 * 1024),
        cost_estimate=pl.CostEstimate(flops=flops, bytes_accessed=size, transcendentals=0),
    )(*scalars, *arrays)


def shape(dims, dtype=BF16):
    return jax.ShapeDtypeStruct(dims, dtype)


def iota(dims, axis):
    return lax.broadcasted_iota(jnp.int32, dims, axis)


def factor_of(ids, ranks, tile, width):
    count = ranks[ids[tile]]
    scale = 2.0 / jnp.full((1, width), count, jnp.int32).astype(F32)
    return jnp.where(iota((1, width), 1) < count * RANK_TILE, scale, 0.0)


def ids_of(ids, n, per, q):
    out = jnp.zeros(q.shape, jnp.int32)
    for i in range(n):
        out = jnp.where(q // per == i, ids[i], out)
    return out


def onehot(mask):
    return mask.astype(F32).astype(BF16)


def up_pack_kernel(ids, up, blocks):
    tiles, rows, lanes = blocks.shape
    q = iota((tiles * rows, up.shape[0]), 0)
    match = ids_of(ids, tiles, rows, q) == iota(q.shape, 1)
    packed = jnp.zeros((tiles * rows, lanes), F32)
    for r in range(rows):
        pick = onehot(match & (q % rows == r))
        packed = packed + dot(pick, up[:, lanes * r : lanes * (r + 1)], 1, 0)
    blocks[...] = packed.astype(BF16).reshape(blocks.shape)


def pack_kernel(meta, ids, down, blocks):
    rank = down.shape[1]
    for chip in range(blocks.shape[0]):
        for slot in range(2):
            adapter = ids[2 * chip + jnp.bitwise_xor(meta[1], slot)]
            blocks[chip, rank * slot : rank * (slot + 1), :] = down[adapter]


def lane_masks(out_width, width, rank):
    per_row = width // rank
    lane_ok = iota((out_width, width), 1) // rank == iota((out_width, width), 0) % per_row
    fold = (iota((width, rank), 0) % rank == iota((width, rank), 1)).astype(F32).astype(BF16)
    return lane_ok, fold


def backward_kernel(meta, ids, ranks, og, packed, up_out, back):
    tiles, rows, lanes = packed.shape
    out_width = og.shape[1]
    rank = back.shape[1]
    flat = packed[...].reshape(tiles * rows, lanes)
    lane_ok, fold = lane_masks(out_width, lanes, rank)
    q = iota((out_width, tiles * rows), 1)
    pick = onehot(iota(q.shape, 0) // (lanes // rank) == q)
    spread = jnp.where(lane_ok, dot(pick, flat, 1, 0), 0.0).astype(BF16)
    up = dot(spread, fold, 1, 0).astype(BF16)
    up_out[...] = up
    factor = factor_of(ids, ranks, 2 * meta[0] + meta[1], rank)
    back[...] = (dot(og[...], up, 1, 0) * factor).astype(BF16)


def grad_kernel(meta, tok_own, tok_sib, back_own, back_sib, grads_own, grads_sib):
    chips, rank, width = grads_own.shape
    pairs_of = ((tok_own, back_own, grads_own), (tok_sib, back_sib, grads_sib))
    for tok, back, grads in pairs_of:
        turned = back[...].T
        for i in range(chips):
            start = pl.multiple_of((2 * i + meta[1]) * width, width)
            term = dot(turned, tok[:, pl.ds(start, width)], 1, 0)
            grads[i, 0:rank, :] = term.astype(BF16)


def low_kernel(meta, tok_own, tok_sib, blocks, low):
    chips, _, width = blocks.shape
    rows = tok_own.shape[0]
    rank = low.shape[1]
    for slot, tok in enumerate((tok_own, tok_sib)):
        total = jnp.zeros((rows, rank), F32)
        for i in range(chips):
            start = pl.multiple_of((2 * i + meta[1]) * width, width)
            part = tok[:, pl.ds(start, width)]
            total = total + dot(part, blocks[i, rank * slot : rank * (slot + 1), :], 1, 1)
        low[rows * slot : rows * (slot + 1), :] = total


def hidden_kernel(meta, ids, ranks, low, other, og_own, og_sib, up, grads, out_low, terms):
    chips, _, width = terms.shape
    rows, out_width = og_own.shape
    rank = up.shape[1]
    k, c = meta[0], meta[1]
    heads = out_width // (2 * chips)
    per_row = width // rank
    q = iota((chips * 16, out_width), 0)
    o = iota((chips * 16, out_width), 1)
    place = o // per_row == (2 * (q // 16) + c) * (heads // per_row) + q % 4
    lane_ok, fold = lane_masks(out_width, width, rank)
    packed = jnp.zeros((chips * 16, width), F32)
    for slot, og in enumerate((og_own, og_sib)):
        factor = factor_of(ids, ranks, 2 * k + jnp.bitwise_xor(c, slot), rank)
        total = low[rows * slot : rows * (slot + 1), :] + other[rows * (1 - slot) : rows * (2 - slot), :]
        hidden = (total * factor).astype(BF16)
        if slot == 0:
            out_low[...] = dot(hidden, up[...], 1, 1)
        term = dot(og[...], hidden, 0, 0).astype(BF16)
        spread = jnp.where(lane_ok, dot(term, fold, 1, 1), 0.0).astype(BF16)
        pick = onehot(place & ((q // 4) % 4 == slot))
        packed = packed + dot(pick, spread, 1, 0)
    terms[...] = packed.astype(BF16).reshape(terms.shape)


def base_kernel(plan, meta, tok_own, tok_sib, og_own, og_sib, back_own, back_sib, blocks, *refs):
    pieces = refs[: len(refs) - 4]
    for_own, for_sib, grad_own, grad_sib = refs[len(refs) - 4 :]
    width = blocks.shape[2]
    rank = back_own.shape[1]
    rows = tok_own.shape[0]
    k, c, g = meta[0], meta[1], meta[2]
    og = jnp.concatenate([og_own[...], og_sib[...]], axis=0)
    total = jnp.zeros((2 * rows, og.shape[1]), F32)
    for index, j, count, side in plan:
        piece = pieces[index]
        chip = jnp.bitwise_xor(k, j)
        shift = 0 if side is None else jnp.bitwise_xor(g, side) * count
        if piece.shape[0] > count:
            weight = piece[pl.ds(pl.multiple_of(chip * count, count), count), :]
        else:
            weight = piece[...]
        start = pl.multiple_of((2 * chip + c) * width + shift, 128)
        tok = jnp.concatenate(
            [tok_own[:, pl.ds(start, count)], tok_sib[:, pl.ds(start, count)]], axis=0
        )
        total = total + dot(tok, weight, 1, 0)
        grad = dot(og, weight, 1, 1)
        inner = pl.ds(pl.multiple_of(shift, 128), count)
        low_own = dot(back_own[...], blocks[chip, 0:rank, inner], 1, 0).astype(BF16)
        low_sib = dot(back_sib[...], blocks[chip, rank : 2 * rank, inner], 1, 0).astype(BF16)
        to = pl.ds(pl.multiple_of(chip * width + shift, 128), count)
        grad_own[:, to] = (grad[:rows] + low_own.astype(F32)).astype(BF16)
        grad_sib[:, to] = (grad[rows:] + low_sib.astype(F32)).astype(BF16)
    for_own[...] = total[:rows]
    for_sib[...] = total[rows:]


def join_kernel(chips, meta, mine, other, out_low, grad_mine, grad_other, result, grad_in):
    c = meta[1]
    result[...] = (mine[...] + other[...] + out_low[...]).astype(BF16)
    width = grad_mine.shape[1] // chips
    for chip in range(chips):
        cols = slice(width * chip, width * (chip + 1))
        own = pl.multiple_of((2 * chip + c) * width, width)
        sib = pl.multiple_of((2 * chip + 1 - c) * width, width)
        grad_in[:, pl.ds(own, width)] = grad_mine[:, cols]
        grad_in[:, pl.ds(sib, width)] = grad_other[:, cols]


def back_kernel(meta, ids, first, second, down_out, up_out):
    rank = down_out.shape[1]
    chips, _, width = first.shape
    c = meta[1]
    flat = jnp.concatenate([second[i, rank : rank + 16, :] for i in range(chips)], axis=0)
    q = iota((up_out.shape[0], chips * 16), 1)
    chosen = jnp.full(q.shape, -1, jnp.int32)
    for chip in range(chips):
        for slot, back in enumerate((first, second)):
            adapter = ids[2 * chip + jnp.bitwise_xor(c, slot)]
            down_out[adapter] = back[chip, 0:rank, :]
            chosen = jnp.where(q // 4 == 4 * chip + slot, adapter, chosen)
    match = chosen == iota(q.shape, 0)
    for r in range(4):
        pick = onehot(match & (q % 4 == r))
        up_out[:, width * r : width * (r + 1)] = dot(pick, flat, 1, 0).astype(BF16)


def after(x, *others):
    return lax.optimization_barrier((x, *others))[0]


def pairs(groups, size, to):
    out = []
    for g in range(groups):
        for d in range(size):
            target = to(g, d)
            if target is not None:
                out.append((g * size + d, target[0] * size + target[1]))
    return out


def gather_weight(weight, groups, size, send, ready):
    chips = size // 2
    rows = weight.shape[0]
    if groups != 2 or chips != 8:
        lists = [[2 * chip + core for chip in range(chips)] for core in range(2)]
        full = lax.all_gather(weight, "dp", axis=0, tiled=True, axis_index_groups=lists)
        return [full], [(0, j, rows, None) for j in range(chips)], (), ()
    half = rows // 2
    mine = lax.dynamic_slice_in_dim(weight, lax.axis_index("groups") * half, half)
    swap_x = lambda g, d: (1 - g, d)
    swap_y = lambda g, d: (g, d ^ 2)
    far = send(mine, lambda g, d: (g, d ^ 12))
    near = send(mine, lambda g, d: (g, d ^ 4))
    own_y = send(after(weight, mine), swap_y)
    far_near = send(after(far, *ready), lambda g, d: (g, d ^ 4))
    arrays = [weight, own_y]
    plan = [(0, 0, rows, None), (1, 1, rows, None)]
    for j, held in ((2, near), (6, far), (4, far_near)):
        over_y = send(held, swap_y)
        first = len(arrays)
        arrays += [held, send(held, swap_x), over_y, send(over_y, swap_x)]
        plan += [(first + i, j + i // 2, half, i % 2) for i in range(4)]
    return arrays, plan, (own_y, near, far), (arrays[4], arrays[8], arrays[12], arrays[3], arrays[7], arrays[9])


def body(groups, size, tokens, out_grad, base_weight, adapter_down, adapter_up, rank_tiles, tile_adapter):
    chips = size // 2
    rows, model_width = tokens.shape
    out_width = out_grad.shape[1]
    adapters, rank, width = adapter_down.shape
    ids = tile_adapter[:, 0]
    place = lax.axis_index("dp")
    meta = jnp.stack([place // 2, place % 2, lax.axis_index("groups")]).astype(jnp.int32)

    def send(x, to):
        return lax.ppermute(x, AXES, pairs(groups, size, to))

    def sibling(x):
        return send(x, lambda g, d: (g, d ^ 1))

    same_core = [[2 * chip + core for chip in range(chips)] for core in range(2)]

    def exchange(blocks):
        return lax.all_to_all(
            blocks, "dp", split_axis=0, concat_axis=0, tiled=True, axis_index_groups=same_core
        )

    tok_sib = sibling(tokens)
    og_sib = sibling(out_grad)
    up_rows = adapter_up.shape[1] // 128
    (up_packed,) = call(up_pack_kernel, [shape((size, up_rows, 128))], (ids,), (adapter_up,))
    up_parts = lax.all_to_all(up_packed, "dp", split_axis=0, concat_axis=0, tiled=True)
    up_mine, back_own = call(
        backward_kernel,
        [shape((out_width, rank)), shape((rows, rank))],
        (meta, ids, rank_tiles),
        (out_grad, up_parts),
    )
    back_sib = sibling(back_own)
    grads_own, grads_sib = call(
        grad_kernel,
        [shape((chips, rank, width)), shape((chips, rank + 16, width))],
        (meta,),
        (tokens, tok_sib, back_own, back_sib),
        flops=2 * rows * model_width * rank,
    )

    (packed,) = call(pack_kernel, [shape((chips, 2 * rank, width))], (meta, ids), (adapter_down,))
    weights, plan, first, early = gather_weight(
        base_weight, groups, size, send, (packed, up_parts)
    )
    blocks = exchange(after(packed, up_parts, tok_sib, og_sib, *first))
    first_back = exchange(after(grads_own, blocks, *early))
    (low,) = call(
        low_kernel,
        [shape((2 * rows, rank), F32)],
        (meta,),
        (tokens, tok_sib, blocks),
        flops=2 * rows * model_width * rank,
    )
    size_up = pl.BlockSpec((chips, 16, width), lambda i: (0, rank // 16, 0))
    out_low, grads_sib = pl.pallas_call(
        hidden_kernel,
        grid=(1,),
        out_shape=[shape((rows, out_width), F32), shape(grads_sib.shape)],
        in_specs=[SMEM] * 3 + [VMEM] * 5 + [pl.BlockSpec(memory_space=pl.ANY)],
        out_specs=[pl.BlockSpec((rows, out_width), lambda i: (0, 0)), size_up],
        input_output_aliases={8: 1},
        compiler_params=pltpu.CompilerParams(vmem_limit_bytes=30 * 1024 * 1024),
    )(meta, ids, rank_tiles, low, sibling(low), out_grad, og_sib, up_mine, grads_sib)
    second_back = exchange(after(grads_sib, first_back))

    for_own, for_sib, grad_own, grad_sib = call(
        functools.partial(base_kernel, plan),
        [shape((rows, out_width), F32)] * 2 + [shape((rows, model_width // 2))] * 2,
        (meta,),
        (tokens, tok_sib, out_grad, og_sib, after(back_own, out_low), back_sib, blocks, *weights),
        flops=4 * rows * model_width * out_width,
        room=60,
    )
    for_other, grad_other = sibling(for_sib), sibling(grad_sib)
    result, grad_in = call(
        functools.partial(join_kernel, chips),
        [shape((rows, out_width)), shape((rows, model_width))],
        (meta,),
        (for_own, for_other, out_low, grad_own, grad_other),
    )
    down_grad, up_grad = call(
        back_kernel,
        [shape(adapter_down.shape), shape(adapter_up.shape)],
        (meta, ids),
        (first_back, second_back),
    )
    return result, grad_in, down_grad, up_grad


def solution(mesh):
    return jax.shard_map(
        functools.partial(body, mesh.shape["groups"], mesh.shape["dp"]),
        mesh=mesh,
        in_specs=(
            P(("groups", "dp"), None),
            P(("groups", "dp"), None),
            P("dp", None),
            P(None, None, "dp"),
            P(None, "dp"),
            P(),
            P("groups", None),
        ),
        out_specs=(
            P(("groups", "dp"), None),
            P(("groups", "dp"), None),
            P("groups", None, "dp"),
            P("groups", "dp"),
        ),
        check_vma=False,
    )
```

```python
import functools

import jax
import jax.numpy as jnp
from jax import lax
from jax.experimental import pallas as pl
from jax.experimental.pallas import tpu as pltpu
from jax.sharding import PartitionSpec as P

RANK_TILE = 16
AXES = ("groups", "dp")
F32 = jnp.float32
BF16 = jnp.bfloat16
VMEM = pl.BlockSpec(memory_space=pltpu.VMEM)
SMEM = pl.BlockSpec(memory_space=pltpu.SMEM)
HBM = pl.BlockSpec(memory_space=pltpu.HBM)


def dot(a, b, ca, cb):
    return lax.dot_general(a, b, (((ca,), (cb,)), ((), ())), preferred_element_type=F32)


def call(kernel, outs, scalars, arrays, flops=0, room=30):
    size = sum(x.size * x.dtype.itemsize for x in arrays)
    size += sum(x.size * x.dtype.itemsize for x in outs)
    return pl.pallas_call(
        kernel,
        out_shape=outs,
        in_specs=[SMEM] * len(scalars) + [VMEM] * len(arrays),
        out_specs=[VMEM] * len(outs),
        compiler_params=pltpu.CompilerParams(vmem_limit_bytes=room * 1024 * 1024),
        cost_estimate=pl.CostEstimate(flops=flops, bytes_accessed=size, transcendentals=0),
    )(*scalars, *arrays)


def shape(dims, dtype=BF16):
    return jax.ShapeDtypeStruct(dims, dtype)


def iota(dims, axis):
    return lax.broadcasted_iota(jnp.int32, dims, axis)


def factor_of(ids, ranks, tile, width):
    count = ranks[ids[tile]]
    scale = 2.0 / jnp.full((1, width), count, jnp.int32).astype(F32)
    return jnp.where(iota((1, width), 1) < count * RANK_TILE, scale, 0.0)


def ids_of(ids, n, per, q):
    out = jnp.zeros(q.shape, jnp.int32)
    for i in range(n):
        out = jnp.where(q // per == i, ids[i], out)
    return out


def onehot(mask):
    return mask.astype(F32).astype(BF16)


def up_pack_kernel(ids, up, blocks):
    tiles, rows, lanes = blocks.shape
    q = iota((tiles * rows, up.shape[0]), 0)
    match = ids_of(ids, tiles, rows, q) == iota(q.shape, 1)
    packed = jnp.zeros((tiles * rows, lanes), F32)
    for r in range(rows):
        pick = onehot(match & (q % rows == r))
        packed = packed + dot(pick, up[:, lanes * r : lanes * (r + 1)], 1, 0)
    blocks[...] = packed.astype(BF16).reshape(blocks.shape)


def pack_kernel(meta, ids, down, blocks):
    rank = down.shape[1]
    for chip in range(blocks.shape[0]):
        for slot in range(2):
            adapter = ids[2 * chip + jnp.bitwise_xor(meta[1], slot)]
            blocks[chip, rank * slot : rank * (slot + 1), :] = down[adapter]


def lane_masks(out_width, width, rank):
    per_row = width // rank
    lane_ok = iota((out_width, width), 1) // rank == iota((out_width, width), 0) % per_row
    fold = (iota((width, rank), 0) % rank == iota((width, rank), 1)).astype(F32).astype(BF16)
    return lane_ok, fold


def backward_kernel(meta, ids, ranks, og, packed, up_out, back):
    tiles, rows, lanes = packed.shape
    out_width = og.shape[1]
    rank = back.shape[1]
    flat = packed[...].reshape(tiles * rows, lanes)
    lane_ok, fold = lane_masks(out_width, lanes, rank)
    q = iota((out_width, tiles * rows), 1)
    pick = onehot(iota(q.shape, 0) // (lanes // rank) == q)
    spread = jnp.where(lane_ok, dot(pick, flat, 1, 0), 0.0).astype(BF16)
    up = dot(spread, fold, 1, 0).astype(BF16)
    up_out[...] = up
    factor = factor_of(ids, ranks, 2 * meta[0] + meta[1], rank)
    back[...] = (dot(og[...], up, 1, 0) * factor).astype(BF16)


def grad_kernel(meta, tok_own, tok_sib, back_own, back_sib, grads_own, grads_sib):
    chips, rank, width = grads_own.shape
    pairs_of = ((tok_own, back_own, grads_own), (tok_sib, back_sib, grads_sib))
    for tok, back, grads in pairs_of:
        turned = back[...].T
        for i in range(chips):
            start = pl.multiple_of((2 * i + meta[1]) * width, width)
            term = dot(turned, tok[:, pl.ds(start, width)], 1, 0)
            grads[i, 0:rank, :] = term.astype(BF16)


def low_kernel(meta, tok_own, tok_sib, blocks, low):
    chips, _, width = blocks.shape
    rows = tok_own.shape[0]
    rank = low.shape[1]
    for slot, tok in enumerate((tok_own, tok_sib)):
        total = jnp.zeros((rows, rank), F32)
        for i in range(chips):
            start = pl.multiple_of((2 * i + meta[1]) * width, width)
            part = tok[:, pl.ds(start, width)]
            total = total + dot(part, blocks[i, rank * slot : rank * (slot + 1), :], 1, 1)
        low[rows * slot : rows * (slot + 1), :] = total


def hidden_kernel(meta, ids, ranks, low, other, og_own, og_sib, up, grads, out_low, terms):
    chips, _, width = terms.shape
    rows, out_width = og_own.shape
    rank = up.shape[1]
    k, c = meta[0], meta[1]
    heads = out_width // (2 * chips)
    per_row = width // rank
    q = iota((chips * 16, out_width), 0)
    o = iota((chips * 16, out_width), 1)
    place = o // per_row == (2 * (q // 16) + c) * (heads // per_row) + q % 4
    lane_ok, fold = lane_masks(out_width, width, rank)
    packed = jnp.zeros((chips * 16, width), F32)
    for slot, og in enumerate((og_own, og_sib)):
        factor = factor_of(ids, ranks, 2 * k + jnp.bitwise_xor(c, slot), rank)
        total = low[rows * slot : rows * (slot + 1), :] + other[rows * (1 - slot) : rows * (2 - slot), :]
        hidden = (total * factor).astype(BF16)
        if slot == 0:
            out_low[...] = dot(hidden, up[...], 1, 1)
        term = dot(og[...], hidden, 0, 0).astype(BF16)
        spread = jnp.where(lane_ok, dot(term, fold, 1, 1), 0.0).astype(BF16)
        pick = onehot(place & ((q // 4) % 4 == slot))
        packed = packed + dot(pick, spread, 1, 0)
    terms[...] = packed.astype(BF16).reshape(terms.shape)


def base_kernel(plan, meta, tok_own, tok_sib, og_own, og_sib, back_own, back_sib, blocks, *refs):
    pieces = refs[: len(refs) - 4]
    for_own, for_sib, grad_own, grad_sib = refs[len(refs) - 4 :]
    width = blocks.shape[2]
    rank = back_own.shape[1]
    rows = tok_own.shape[0]
    k, c, g = meta[0], meta[1], meta[2]
    og = jnp.concatenate([og_own[...], og_sib[...]], axis=0)
    total = jnp.zeros((2 * rows, og.shape[1]), F32)
    for index, j, count, side in plan:
        piece = pieces[index]
        chip = jnp.bitwise_xor(k, j)
        shift = 0 if side is None else jnp.bitwise_xor(g, side) * count
        if piece.shape[0] > count:
            weight = piece[pl.ds(pl.multiple_of(chip * count, count), count), :]
        else:
            weight = piece[...]
        start = pl.multiple_of((2 * chip + c) * width + shift, 128)
        tok = jnp.concatenate(
            [tok_own[:, pl.ds(start, count)], tok_sib[:, pl.ds(start, count)]], axis=0
        )
        total = total + dot(tok, weight, 1, 0)
        grad = dot(og, weight, 1, 1)
        inner = pl.ds(pl.multiple_of(shift, 128), count)
        low_own = dot(back_own[...], blocks[chip, 0:rank, inner], 1, 0).astype(BF16)
        low_sib = dot(back_sib[...], blocks[chip, rank : 2 * rank, inner], 1, 0).astype(BF16)
        to = pl.ds(pl.multiple_of(chip * width + shift, 128), count)
        grad_own[:, pl.ds(start, count)] = (grad[:rows] + low_own.astype(F32)).astype(BF16)
        grad_sib[:, to] = (grad[rows:] + low_sib.astype(F32)).astype(BF16)
    for_own[...] = total[:rows]
    for_sib[...] = total[rows:]


def join_kernel(chips, meta, mine, other, out_low, grad_other, grad_mine, result, grad_in, sems):
    width = grad_other.shape[1] // chips
    copies = []
    for chip in range(chips):
        to = pl.ds(pl.multiple_of((2 * chip + 1 - meta[1]) * width, width), width)
        copies.append(
            pltpu.make_async_copy(
                grad_other.at[:, width * chip : width * (chip + 1)],
                grad_in.at[:, to],
                sems.at[chip],
            )
        )
        copies[chip].start()
    result[...] = (mine[...] + other[...] + out_low[...]).astype(BF16)
    for copy in copies:
        copy.wait()


def back_kernel(meta, ids, first, second, down_out, up_out):
    rank = down_out.shape[1]
    chips, _, width = first.shape
    c = meta[1]
    flat = jnp.concatenate([second[i, rank : rank + 16, :] for i in range(chips)], axis=0)
    q = iota((up_out.shape[0], chips * 16), 1)
    chosen = jnp.full(q.shape, -1, jnp.int32)
    for chip in range(chips):
        for slot, back in enumerate((first, second)):
            adapter = ids[2 * chip + jnp.bitwise_xor(c, slot)]
            down_out[adapter] = back[chip, 0:rank, :]
            chosen = jnp.where(q // 4 == 4 * chip + slot, adapter, chosen)
    match = chosen == iota(q.shape, 0)
    for r in range(4):
        pick = onehot(match & (q % 4 == r))
        up_out[:, width * r : width * (r + 1)] = dot(pick, flat, 1, 0).astype(BF16)


def after(x, *others):
    return lax.optimization_barrier((x, *others))[0]


def pairs(groups, size, to):
    out = []
    for g in range(groups):
        for d in range(size):
            target = to(g, d)
            if target is not None:
                out.append((g * size + d, target[0] * size + target[1]))
    return out


def gather_weight(weight, groups, size, send, ready):
    chips = size // 2
    rows = weight.shape[0]
    if groups != 2 or chips != 8:
        lists = [[2 * chip + core for chip in range(chips)] for core in range(2)]
        full = lax.all_gather(weight, "dp", axis=0, tiled=True, axis_index_groups=lists)
        return [full], [(0, j, rows, None) for j in range(chips)], (), ()
    half = rows // 2
    mine = lax.dynamic_slice_in_dim(weight, lax.axis_index("groups") * half, half)
    swap_x = lambda g, d: (1 - g, d)
    swap_y = lambda g, d: (g, d ^ 2)
    far = send(mine, lambda g, d: (g, d ^ 12))
    near = send(mine, lambda g, d: (g, d ^ 4))
    own_y = send(after(weight, mine), swap_y)
    far_near = send(after(far, *ready), lambda g, d: (g, d ^ 4))
    arrays = [weight, own_y]
    plan = [(0, 0, rows, None), (1, 1, rows, None)]
    for j, held in ((2, near), (6, far), (4, far_near)):
        over_y = send(held, swap_y)
        first = len(arrays)
        arrays += [held, send(held, swap_x), over_y, send(over_y, swap_x)]
        plan += [(first + i, j + i // 2, half, i % 2) for i in range(4)]
    return arrays, plan, (own_y, near, far), (arrays[4], arrays[8], arrays[12], arrays[3], arrays[7], arrays[9])


def body(groups, size, tokens, out_grad, base_weight, adapter_down, adapter_up, rank_tiles, tile_adapter):
    chips = size // 2
    rows, model_width = tokens.shape
    out_width = out_grad.shape[1]
    adapters, rank, width = adapter_down.shape
    ids = tile_adapter[:, 0]
    place = lax.axis_index("dp")
    meta = jnp.stack([place // 2, place % 2, lax.axis_index("groups")]).astype(jnp.int32)

    def send(x, to):
        return lax.ppermute(x, AXES, pairs(groups, size, to))

    def sibling(x):
        return send(x, lambda g, d: (g, d ^ 1))

    same_core = [[2 * chip + core for chip in range(chips)] for core in range(2)]

    def exchange(blocks):
        return lax.all_to_all(
            blocks, "dp", split_axis=0, concat_axis=0, tiled=True, axis_index_groups=same_core
        )

    tok_sib = sibling(tokens)
    og_sib = sibling(out_grad)
    up_rows = adapter_up.shape[1] // 128
    (up_packed,) = call(up_pack_kernel, [shape((size, up_rows, 128))], (ids,), (adapter_up,))
    up_parts = lax.all_to_all(up_packed, "dp", split_axis=0, concat_axis=0, tiled=True)
    up_mine, back_own = call(
        backward_kernel,
        [shape((out_width, rank)), shape((rows, rank))],
        (meta, ids, rank_tiles),
        (out_grad, up_parts),
    )
    back_sib = sibling(back_own)
    grads_own, grads_sib = call(
        grad_kernel,
        [shape((chips, rank, width)), shape((chips, rank + 16, width))],
        (meta,),
        (tokens, tok_sib, back_own, back_sib),
        flops=2 * rows * model_width * rank,
    )

    (packed,) = call(pack_kernel, [shape((chips, 2 * rank, width))], (meta, ids), (adapter_down,))
    weights, plan, first, early = gather_weight(
        base_weight, groups, size, send, (up_packed,)
    )
    blocks = exchange(after(packed, up_parts, tok_sib, og_sib, *first))
    first_back = exchange(after(grads_own, blocks, *early))
    (low,) = call(
        low_kernel,
        [shape((2 * rows, rank), F32)],
        (meta,),
        (tokens, tok_sib, blocks),
        flops=2 * rows * model_width * rank,
    )
    size_up = pl.BlockSpec((chips, 16, width), lambda i: (0, rank // 16, 0))
    out_low, grads_sib = pl.pallas_call(
        hidden_kernel,
        grid=(1,),
        out_shape=[shape((rows, out_width), F32), shape(grads_sib.shape)],
        in_specs=[SMEM] * 3 + [VMEM] * 5 + [pl.BlockSpec(memory_space=pl.ANY)],
        out_specs=[pl.BlockSpec((rows, out_width), lambda i: (0, 0)), size_up],
        input_output_aliases={8: 1},
        compiler_params=pltpu.CompilerParams(vmem_limit_bytes=30 * 1024 * 1024),
    )(meta, ids, rank_tiles, low, sibling(low), out_grad, og_sib, up_mine, grads_sib)
    second_back = exchange(after(grads_sib, first_back))

    for_own, for_sib, grad_own, grad_sib = call(
        functools.partial(base_kernel, plan),
        [shape((rows, out_width), F32)] * 2
        + [shape((rows, model_width)), shape((rows, model_width // 2))],
        (meta,),
        (tokens, tok_sib, out_grad, og_sib, after(back_own, out_low), back_sib, blocks, *weights),
        flops=4 * rows * model_width * out_width,
        room=60,
    )
    for_other, grad_other = sibling(for_sib), sibling(grad_sib)
    result, grad_in = pl.pallas_call(
        functools.partial(join_kernel, chips),
        out_shape=[shape((rows, out_width)), shape((rows, model_width))],
        in_specs=[SMEM] + [VMEM] * 3 + [HBM] * 2,
        out_specs=[VMEM, HBM],
        scratch_shapes=[pltpu.SemaphoreType.DMA((chips,))],
        input_output_aliases={5: 1},
        compiler_params=pltpu.CompilerParams(vmem_limit_bytes=30 * 1024 * 1024),
    )(meta, for_own, for_other, out_low, grad_other, grad_own)
    down_grad, up_grad = call(
        back_kernel,
        [shape(adapter_down.shape), shape(adapter_up.shape)],
        (meta, ids),
        (first_back, second_back),
    )
    return result, grad_in, down_grad, up_grad


def solution(mesh):
    return jax.shard_map(
        functools.partial(body, mesh.shape["groups"], mesh.shape["dp"]),
        mesh=mesh,
        in_specs=(
            P(("groups", "dp"), None),
            P(("groups", "dp"), None),
            P("dp", None),
            P(None, None, "dp"),
            P(None, "dp"),
            P(),
            P("groups", None),
        ),
        out_specs=(
            P(("groups", "dp"), None),
            P(("groups", "dp"), None),
            P("groups", None, "dp"),
            P("groups", "dp"),
        ),
        check_vma=False,
    )
```

```python
import functools

import jax
import jax.numpy as jnp
from jax import lax
from jax.experimental import pallas as pl
from jax.experimental.pallas import tpu as pltpu
from jax.sharding import PartitionSpec as P

RANK_TILE = 16
AXES = ("groups", "dp")
F32 = jnp.float32
BF16 = jnp.bfloat16
VMEM = pl.BlockSpec(memory_space=pltpu.VMEM)
SMEM = pl.BlockSpec(memory_space=pltpu.SMEM)
HBM = pl.BlockSpec(memory_space=pltpu.HBM)


def dot(a, b, ca, cb):
    return lax.dot_general(a, b, (((ca,), (cb,)), ((), ())), preferred_element_type=F32)


def call(kernel, outs, scalars, arrays, flops=0, room=30):
    size = sum(x.size * x.dtype.itemsize for x in arrays)
    size += sum(x.size * x.dtype.itemsize for x in outs)
    return pl.pallas_call(
        kernel,
        out_shape=outs,
        in_specs=[SMEM] * len(scalars) + [VMEM] * len(arrays),
        out_specs=[VMEM] * len(outs),
        compiler_params=pltpu.CompilerParams(vmem_limit_bytes=room * 1024 * 1024),
        cost_estimate=pl.CostEstimate(flops=flops, bytes_accessed=size, transcendentals=0),
    )(*scalars, *arrays)


def shape(dims, dtype=BF16):
    return jax.ShapeDtypeStruct(dims, dtype)


def iota(dims, axis):
    return lax.broadcasted_iota(jnp.int32, dims, axis)


def factor_of(ids, ranks, tile, width):
    count = ranks[ids[tile]]
    scale = 2.0 / jnp.full((1, width), count, jnp.int32).astype(F32)
    return jnp.where(iota((1, width), 1) < count * RANK_TILE, scale, 0.0)


def ids_of(ids, n, per, q):
    out = jnp.zeros(q.shape, jnp.int32)
    for i in range(n):
        out = jnp.where(q // per == i, ids[i], out)
    return out


def onehot(mask):
    return mask.astype(F32).astype(BF16)


def up_pack_kernel(ids, up, blocks):
    tiles, rows, lanes = blocks.shape
    q = iota((tiles * rows, up.shape[0]), 0)
    match = ids_of(ids, tiles, rows, q) == iota(q.shape, 1)
    packed = jnp.zeros((tiles * rows, lanes), F32)
    for r in range(rows):
        pick = onehot(match & (q % rows == r))
        packed = packed + dot(pick, up[:, lanes * r : lanes * (r + 1)], 1, 0)
    blocks[...] = packed.astype(BF16).reshape(blocks.shape)


def pack_kernel(meta, ids, down, blocks):
    rank = down.shape[1]
    for chip in range(blocks.shape[0]):
        for slot in range(2):
            adapter = ids[2 * chip + jnp.bitwise_xor(meta[1], slot)]
            blocks[chip, rank * slot : rank * (slot + 1), :] = down[adapter]


def lane_masks(out_width, width, rank):
    per_row = width // rank
    lane_ok = iota((out_width, width), 1) // rank == iota((out_width, width), 0) % per_row
    fold = (iota((width, rank), 0) % rank == iota((width, rank), 1)).astype(F32).astype(BF16)
    return lane_ok, fold


def backward_kernel(meta, ids, ranks, og, packed, up_out, back):
    tiles, rows, lanes = packed.shape
    out_width = og.shape[1]
    rank = back.shape[1]
    flat = packed[...].reshape(tiles * rows, lanes)
    lane_ok, fold = lane_masks(out_width, lanes, rank)
    q = iota((out_width, tiles * rows), 1)
    pick = onehot(iota(q.shape, 0) // (lanes // rank) == q)
    spread = jnp.where(lane_ok, dot(pick, flat, 1, 0), 0.0).astype(BF16)
    up = dot(spread, fold, 1, 0).astype(BF16)
    up_out[...] = up
    factor = factor_of(ids, ranks, 2 * meta[0] + meta[1], rank)
    back[...] = (dot(og[...], up, 1, 0) * factor).astype(BF16)


def grad_kernel(meta, tok_own, tok_sib, back_own, back_sib, grads_own, grads_sib):
    chips, rank, width = grads_own.shape
    pairs_of = ((tok_own, back_own, grads_own), (tok_sib, back_sib, grads_sib))
    for tok, back, grads in pairs_of:
        turned = back[...].T
        for i in range(chips):
            start = pl.multiple_of((2 * i + meta[1]) * width, width)
            term = dot(turned, tok[:, pl.ds(start, width)], 1, 0)
            grads[i, 0:rank, :] = term.astype(BF16)


def low_kernel(meta, tok_own, tok_sib, blocks, low):
    chips, _, width = blocks.shape
    rows = tok_own.shape[0]
    rank = low.shape[1]
    for slot, tok in enumerate((tok_own, tok_sib)):
        total = jnp.zeros((rows, rank), F32)
        for i in range(chips):
            start = pl.multiple_of((2 * i + meta[1]) * width, width)
            part = tok[:, pl.ds(start, width)]
            total = total + dot(part, blocks[i, rank * slot : rank * (slot + 1), :], 1, 1)
        low[rows * slot : rows * (slot + 1), :] = total


def hidden_kernel(meta, ids, ranks, low, other, og_own, og_sib, up, grads, out_low, terms):
    chips, _, width = terms.shape
    rows, out_width = og_own.shape
    rank = up.shape[1]
    k, c = meta[0], meta[1]
    heads = out_width // (2 * chips)
    per_row = width // rank
    q = iota((chips * 16, out_width), 0)
    o = iota((chips * 16, out_width), 1)
    place = o // per_row == (2 * (q // 16) + c) * (heads // per_row) + q % 4
    lane_ok, fold = lane_masks(out_width, width, rank)
    packed = jnp.zeros((chips * 16, width), F32)
    for slot, og in enumerate((og_own, og_sib)):
        factor = factor_of(ids, ranks, 2 * k + jnp.bitwise_xor(c, slot), rank)
        total = low[rows * slot : rows * (slot + 1), :] + other[rows * (1 - slot) : rows * (2 - slot), :]
        hidden = (total * factor).astype(BF16)
        if slot == 0:
            out_low[...] = dot(hidden, up[...], 1, 1)
        term = dot(og[...], hidden, 0, 0).astype(BF16)
        spread = jnp.where(lane_ok, dot(term, fold, 1, 1), 0.0).astype(BF16)
        pick = onehot(place & ((q // 4) % 4 == slot))
        packed = packed + dot(pick, spread, 1, 0)
    terms[...] = packed.astype(BF16).reshape(terms.shape)


def base_kernel(plan, meta, tok_own, tok_sib, og_own, og_sib, back_own, back_sib, blocks, *refs):
    pieces = refs[: len(refs) - 4]
    for_own, for_sib, grad_own, grad_sib = refs[len(refs) - 4 :]
    width = blocks.shape[2]
    rank = back_own.shape[1]
    rows = tok_own.shape[0]
    k, c, g = meta[0], meta[1], meta[2]
    og = jnp.concatenate([og_own[...], og_sib[...]], axis=0)
    total = jnp.zeros((2 * rows, og.shape[1]), F32)
    for index, j, count, side in plan:
        piece = pieces[index]
        chip = jnp.bitwise_xor(k, j)
        shift = 0 if side is None else jnp.bitwise_xor(g, side) * count
        if piece.shape[0] > count:
            weight = piece[pl.ds(pl.multiple_of(chip * count, count), count), :]
        else:
            weight = piece[...]
        start = pl.multiple_of((2 * chip + c) * width + shift, 128)
        tok = jnp.concatenate(
            [tok_own[:, pl.ds(start, count)], tok_sib[:, pl.ds(start, count)]], axis=0
        )
        total = total + dot(tok, weight, 1, 0)
        grad = dot(og, weight, 1, 1)
        inner = pl.ds(pl.multiple_of(shift, 128), count)
        low_own = dot(back_own[...], blocks[chip, 0:rank, inner], 1, 0).astype(BF16)
        low_sib = dot(back_sib[...], blocks[chip, rank : 2 * rank, inner], 1, 0).astype(BF16)
        to = pl.ds(pl.multiple_of(chip * width + shift, 128), count)
        grad_own[:, pl.ds(start, count)] = (grad[:rows] + low_own.astype(F32)).astype(BF16)
        grad_sib[:, to] = (grad[rows:] + low_sib.astype(F32)).astype(BF16)
    for_own[...] = total[:rows]
    for_sib[...] = total[rows:]


def join_kernel(chips, meta, mine, other, out_low, grad_other, grad_mine, result, grad_in, sems):
    width = grad_other.shape[1] // chips
    copies = []
    for chip in range(chips):
        to = pl.ds(pl.multiple_of((2 * chip + 1 - meta[1]) * width, width), width)
        copies.append(
            pltpu.make_async_copy(
                grad_other.at[:, width * chip : width * (chip + 1)],
                grad_in.at[:, to],
                sems.at[chip],
            )
        )
        copies[chip].start()
    result[...] = (mine[...] + other[...] + out_low[...]).astype(BF16)
    for copy in copies:
        copy.wait()


def back_kernel(meta, ids, first, second, down_out, up_out):
    rank = down_out.shape[1]
    chips, _, width = first.shape
    c = meta[1]
    flat = jnp.concatenate([second[i, rank : rank + 16, :] for i in range(chips)], axis=0)
    q = iota((up_out.shape[0], chips * 16), 1)
    chosen = jnp.full(q.shape, -1, jnp.int32)
    for chip in range(chips):
        for slot, back in enumerate((first, second)):
            adapter = ids[2 * chip + jnp.bitwise_xor(c, slot)]
            down_out[adapter] = back[chip, 0:rank, :]
            chosen = jnp.where(q // 4 == 4 * chip + slot, adapter, chosen)
    match = chosen == iota(q.shape, 0)
    for r in range(4):
        pick = onehot(match & (q % 4 == r))
        up_out[:, width * r : width * (r + 1)] = dot(pick, flat, 1, 0).astype(BF16)


def after(x, *others):
    return lax.optimization_barrier((x, *others))[0]


def pairs(groups, size, to):
    out = []
    for g in range(groups):
        for d in range(size):
            target = to(g, d)
            if target is not None:
                out.append((g * size + d, target[0] * size + target[1]))
    return out


def gather_weight(weight, groups, size, send, ready):
    chips = size // 2
    rows = weight.shape[0]
    if groups != 2 or chips != 8:
        lists = [[2 * chip + core for chip in range(chips)] for core in range(2)]
        full = lax.all_gather(weight, "dp", axis=0, tiled=True, axis_index_groups=lists)
        return [full], [(0, j, rows, None) for j in range(chips)], (), ()
    half = rows // 2
    mine = lax.dynamic_slice_in_dim(weight, lax.axis_index("groups") * half, half)
    swap_x = lambda g, d: (1 - g, d)
    swap_y = lambda g, d: (g, d ^ 2)
    far = send(mine, lambda g, d: (g, d ^ 12))
    near = send(mine, lambda g, d: (g, d ^ 4))
    own_y = send(after(weight, mine), swap_y)
    far_near = send(after(far, *ready), lambda g, d: (g, d ^ 4))
    arrays = [weight, own_y]
    plan = [(0, 0, rows, None), (1, 1, rows, None)]
    for j, held in ((2, near), (6, far), (4, far_near)):
        over_y = send(held, swap_y)
        first = len(arrays)
        arrays += [held, send(held, swap_x), over_y, send(over_y, swap_x)]
        plan += [(first + i, j + i // 2, half, i % 2) for i in range(4)]
    return arrays, plan, (own_y, near, far), (arrays[4], arrays[8], arrays[12], arrays[3], arrays[7], arrays[9])


def body(groups, size, tokens, out_grad, base_weight, adapter_down, adapter_up, rank_tiles, tile_adapter):
    chips = size // 2
    rows, model_width = tokens.shape
    out_width = out_grad.shape[1]
    adapters, rank, width = adapter_down.shape
    ids = tile_adapter[:, 0]
    place = lax.axis_index("dp")
    meta = jnp.stack([place // 2, place % 2, lax.axis_index("groups")]).astype(jnp.int32)

    def send(x, to):
        return lax.ppermute(x, AXES, pairs(groups, size, to))

    def sibling(x):
        return send(x, lambda g, d: (g, d ^ 1))

    same_core = [[2 * chip + core for chip in range(chips)] for core in range(2)]

    def exchange(blocks):
        return lax.all_to_all(
            blocks, "dp", split_axis=0, concat_axis=0, tiled=True, axis_index_groups=same_core
        )

    tok_sib = sibling(tokens)
    og_sib = sibling(out_grad)
    up_rows = adapter_up.shape[1] // 128
    (up_packed,) = call(up_pack_kernel, [shape((size, up_rows, 128))], (ids,), (adapter_up,))
    up_parts = lax.all_to_all(up_packed, "dp", split_axis=0, concat_axis=0, tiled=True)
    up_mine, back_own = call(
        backward_kernel,
        [shape((out_width, rank)), shape((rows, rank))],
        (meta, ids, rank_tiles),
        (out_grad, up_parts),
    )
    back_sib = sibling(back_own)
    grads_own, grads_sib = call(
        grad_kernel,
        [shape((chips, rank, width)), shape((chips, rank + 16, width))],
        (meta,),
        (tokens, tok_sib, back_own, back_sib),
        flops=2 * rows * model_width * rank,
    )

    (packed,) = call(pack_kernel, [shape((chips, 2 * rank, width))], (meta, ids), (adapter_down,))
    weights, plan, first, early = gather_weight(
        base_weight, groups, size, send, (up_packed,)
    )
    blocks = exchange(after(packed, tok_sib, og_sib, *first))
    first_back = exchange(after(grads_own, blocks, *early))
    (low,) = call(
        low_kernel,
        [shape((2 * rows, rank), F32)],
        (meta,),
        (tokens, tok_sib, blocks),
        flops=2 * rows * model_width * rank,
    )
    size_up = pl.BlockSpec((chips, 16, width), lambda i: (0, rank // 16, 0))
    out_low, grads_sib = pl.pallas_call(
        hidden_kernel,
        grid=(1,),
        out_shape=[shape((rows, out_width), F32), shape(grads_sib.shape)],
        in_specs=[SMEM] * 3 + [VMEM] * 5 + [pl.BlockSpec(memory_space=pl.ANY)],
        out_specs=[pl.BlockSpec((rows, out_width), lambda i: (0, 0)), size_up],
        input_output_aliases={8: 1},
        compiler_params=pltpu.CompilerParams(vmem_limit_bytes=30 * 1024 * 1024),
    )(meta, ids, rank_tiles, low, sibling(low), out_grad, og_sib, up_mine, grads_sib)
    second_back = exchange(after(grads_sib, first_back))

    for_own, for_sib, grad_own, grad_sib = call(
        functools.partial(base_kernel, plan),
        [shape((rows, out_width), F32)] * 2
        + [shape((rows, model_width)), shape((rows, model_width // 2))],
        (meta,),
        (tokens, tok_sib, out_grad, og_sib, after(back_own, out_low), back_sib, blocks, *weights),
        flops=4 * rows * model_width * out_width,
        room=60,
    )
    for_other, grad_other = sibling(for_sib), sibling(grad_sib)
    result, grad_in = pl.pallas_call(
        functools.partial(join_kernel, chips),
        out_shape=[shape((rows, out_width)), shape((rows, model_width))],
        in_specs=[SMEM] + [VMEM] * 3 + [HBM] * 2,
        out_specs=[VMEM, HBM],
        scratch_shapes=[pltpu.SemaphoreType.DMA((chips,))],
        input_output_aliases={5: 1},
        compiler_params=pltpu.CompilerParams(vmem_limit_bytes=30 * 1024 * 1024),
    )(meta, for_own, for_other, out_low, grad_other, grad_own)
    down_grad, up_grad = call(
        back_kernel,
        [shape(adapter_down.shape), shape(adapter_up.shape)],
        (meta, ids),
        (first_back, second_back),
    )
    return result, grad_in, down_grad, up_grad


def solution(mesh):
    return jax.shard_map(
        functools.partial(body, mesh.shape["groups"], mesh.shape["dp"]),
        mesh=mesh,
        in_specs=(
            P(("groups", "dp"), None),
            P(("groups", "dp"), None),
            P("dp", None),
            P(None, None, "dp"),
            P(None, "dp"),
            P(),
            P("groups", None),
        ),
        out_specs=(
            P(("groups", "dp"), None),
            P(("groups", "dp"), None),
            P("groups", None, "dp"),
            P("groups", "dp"),
        ),
        check_vma=False,
    )
```
